256 devices in a mesh: wide: 64 (over z, y, x_hi), narrow: 4 (over x_lo, core).
Axes of the slice: x: 4 (x_hi: 2, x_lo: 2; x = x_hi * 2 + x_lo), y: 4, z: 8, core: 2. Of those that a mesh axis runs over, the one named last changes fastest.
Arguments:
- embeddings: bfloat16 [65536, 4096], P('wide', 'narrow'), may hold values from -6 to 6
- cluster_ids: int32 [65536, 1], P('wide'), may hold values from 0 to 63; in each aligned block of 1024 rows (0 to 1023, 1024 to 2047, ...) at most 32 rows name the same one
Outputs:
- gram_tiles: bfloat16 [64, 2048, 2048], P('wide', None, 'narrow')
The draws below stay inside these ranges and needn't reach their ends.
Inputs may be any that keep to these rules, and one draw needn't show every extreme that they name: `cluster_ids`: in each aligned block of 1024 rows (the rows of one index of wide), no cluster is named by more than 32 rows, a bound that some block reaches.
All inputs are finite; a program needn't handle non-finite values.
Results may differ from the reference program's by a relative error of at most 0.0075.
Values may be sent and summed in bfloat16 or wider, within the bound.
A program may use at most 64 MiB of HBM per device.

```python
import math
import jax
import jax.numpy as jnp
import numpy as np
from jax import lax

D = 4096
K = 256
ROWS = 1024
ITERS = 2
ROWS_ALL = 65536
CLUSTERS = 64
CAP = 32
MEMBERS = 2048
N_WIDE = 64


def draw_embeddings(key, part):
    first_key = jax.random.fold_in(key, 11)
    third_key = jax.random.fold_in(key, 13)
    fourth_key = jax.random.fold_in(key, 14)
    per_block = K // CLUSTERS
    strength = 4.0 * CLUSTERS ** 0.5
    directions = jnp.clip(jax.random.normal(third_key, (CLUSTERS, per_block, D), jnp.float32), -6.0, 6.0) * D ** (-0.5)
    values = jax.random.normal(first_key, (ROWS_ALL, D), jnp.float32)
    amounts = jnp.clip(jax.random.normal(fourth_key, (CLUSTERS, ROWS, per_block), jnp.float32), -4.0, 4.0) * strength
    planted = jnp.einsum('brp,bpd->brd', amounts, directions).reshape(ROWS_ALL, D)
    return jnp.clip(values + planted, -6.0, 6.0).astype(jnp.bfloat16)


def shared_out(stream_key, own, number, rows, amount, top, limit, slope):
    ranking = jax.random.permutation(stream_key, amount)
    packed, common = load_shares(amount, rows * top, limit, slope, True), load_shares(amount, rows * top, limit, slope, False)
    places = jnp.arange(amount)

    def named(lengths, rotation):
        used = int((lengths > 0).sum())
        fixed = max(1, used // 4)
        shifted = fixed + (places - fixed + rotation * (used - fixed)) % max(1, amount - fixed)
        return jnp.zeros((amount,), jnp.int32).at[ranking[jnp.where(places < fixed, places, shifted)]].set(jnp.asarray(lengths, jnp.int32))

    lengths = jnp.where(number % 4 == 0, named(packed, number // 4), named(common, number - number // 4 - 1))
    mixed = jax.random.permutation(jax.random.fold_in(own, 3), amount)
    giver, sink = mixed[0:amount // 2 * 2:2], mixed[1:amount // 2 * 2:2]
    margin = jnp.minimum(lengths[giver] - 1, limit - lengths[sink]) // 2
    margin = jnp.where((giver == ranking[0]) | (sink == ranking[0]) | (lengths[sink] == 0), 0, jnp.maximum(margin, 0))
    shifted = jax.random.randint(jax.random.fold_in(own, 4), (amount // 2,), 0, 1 << 20) % (margin + 1)
    lengths = lengths.at[giver].add(-shifted).at[sink].add(shifted)
    labels = jnp.searchsorted(jnp.cumsum(lengths), jnp.arange(rows * top), side="right").astype(jnp.int32)
    grid = labels.reshape(top, rows).T
    grid = grid[jax.random.permutation(jax.random.fold_in(own, 1), rows)]
    rotation = jax.random.randint(jax.random.fold_in(own, 2), (rows, 1), 0, top)
    return jnp.take_along_axis(grid, (jnp.arange(top)[None, :] + rotation) % top, axis=1)


def load_shares(count, total, reach, slope, full):
    loads = [(1 << 20) // math.isqrt(grade ** slope) + 1 for grade in range(1, count + 1)]
    largest = reach if full else min(reach, max(-(-total // count), total * loads[0] // sum(loads)))
    least = 1 if total - largest >= count - 1 else 0
    counts, rest = [largest] + [least] * (count - 1), total - largest - least * (count - 1)
    while rest > 0:
        free = [i for i in range(1, count) if counts[i] < largest] or [i for i in range(1, count) if counts[i] < reach]
        pool, budget = sum([loads[i] for i in free]), rest
        for i in free:
            more = min(reach - counts[i], max(1, budget * loads[i] // pool), rest)
            counts[i] = counts[i] + more
            rest = rest - more
    return np.array(counts)


def setup_inputs(seed: int = 0) -> dict:
    key_list = jax.random.split(jax.random.key(seed), 3)
    embeddings = draw_embeddings(jax.random.fold_in(key_list[2], 71), 0)
    cluster_ids_keys = jax.random.split(jax.random.fold_in(key_list[1], 1), ROWS_ALL // ROWS)
    cluster_ids_turns = jax.random.permutation(jax.random.fold_in(key_list[1], 3), ROWS_ALL // ROWS)
    cluster_ids = jax.vmap(lambda own, number: shared_out(jax.random.fold_in(key_list[1], 2), own, number, ROWS, CLUSTERS, 1, CAP, 2))(cluster_ids_keys, cluster_ids_turns).reshape((ROWS_ALL, 1))
    return dict(embeddings=embeddings, cluster_ids=cluster_ids)


def orthonormal(image_rows, square):
    lower_factor = jnp.linalg.cholesky(square)
    return lax.linalg.triangular_solve(lower_factor, image_rows, left_side=False, lower=True, transpose_a=True)

def cluster_gram(block):
    return jnp.dot(block.astype(jnp.float32), block.T.astype(jnp.float32), preferred_element_type=jnp.float32).astype(jnp.bfloat16)

def normalize_rows(coords):
    sum_squares = lax.optimization_barrier(jnp.sum(coords * coords, axis=1, keepdims=True))
    scale_factor = lax.rsqrt(sum_squares + 1e-06)
    return (coords * scale_factor).astype(jnp.bfloat16)

def reference(embeddings, cluster_ids):
    row_pos = jnp.arange(D, dtype=jnp.int32)
    col_pos = jnp.arange(K, dtype=jnp.int32)
    basis_now = (row_pos[:, None] % K == col_pos[None, :]).astype(jnp.float32)
    for sweep in range(ITERS):
        coords = jnp.dot(embeddings.astype(jnp.float32), basis_now.astype(jnp.bfloat16).astype(jnp.float32), preferred_element_type=jnp.float32)
        image_rows = lax.dot_general(embeddings.astype(jnp.float32), coords.astype(jnp.bfloat16).astype(jnp.float32), (((0,), (0,)), ((), ())), preferred_element_type=jnp.float32)
        square = jnp.dot(image_rows.T, image_rows, precision=lax.Precision.HIGHEST)
        basis_now = orthonormal(image_rows, square)
    coords = jnp.dot(embeddings.astype(jnp.float32), basis_now.astype(jnp.bfloat16).astype(jnp.float32), preferred_element_type=jnp.float32)
    unit_rows = normalize_rows(coords)
    owner_ids = cluster_ids[:, 0]
    grouped = owner_ids.reshape(N_WIDE, ROWS)
    onehot = (grouped[:, :, None] == jnp.arange(CLUSTERS, dtype=jnp.int32)[None, None, :]).astype(jnp.int32)
    slot_index = lax.optimization_barrier(jnp.sum((jnp.cumsum(onehot, axis=1) - onehot) * onehot, axis=2)).reshape(-1)
    source = jnp.repeat(jnp.arange(N_WIDE, dtype=jnp.int32), ROWS)
    members = jnp.zeros((CLUSTERS, MEMBERS, K), unit_rows.dtype)
    members = members.at[owner_ids, slot_index * N_WIDE + source].set(unit_rows)
    return lax.map(cluster_gram, members)
```

```python
import jax
import jax.numpy as jnp
from jax import lax
from jax.experimental import pallas as pl
from jax.experimental.pallas import tpu as pltpu
from jax.sharding import PartitionSpec as P

F32 = jnp.float32
BF16 = jnp.bfloat16
HIGHEST = lax.Precision.HIGHEST
MESH = pl.DeviceIdType.MESH

K = 256
ITERS = 2
HALF = 128
PANEL = 16
CHUNKS = 4
WIDE = 64
PIECE = 16
SLOTS = 32


def dot(a, b, dims, precision=None):
    return lax.dot_general(
        a, b, (dims, ((), ())), precision=precision, preferred_element_type=F32
    )


NN = ((1,), (0,))
NT = ((1,), (1,))


def split3(x):
    a = x.astype(BF16)
    rest = x - a.astype(F32)
    b = rest.astype(BF16)
    c = (rest - b.astype(F32)).astype(BF16)
    return a, b, c


def eliminate(m):
    n = HALF
    sub = lax.broadcasted_iota(jnp.int32, (PANEL, n), 0)
    for r0 in range(0, n, PANEL):
        left = m[r0 : r0 + PANEL, 0:n]
        right = m[r0 : r0 + PANEL, n : 2 * n]
        cols = [
            jnp.broadcast_to(left[:, r0 + j : r0 + j + 1], (PANEL, n)) for j in range(PANEL)
        ]
        scale = jnp.zeros((PANEL, n), F32)
        for j in range(PANEL):
            pivot = cols[j][j : j + 1, :]
            factor = jnp.where(sub > j, cols[j] * (1.0 / pivot), 0.0)
            for k in range(j + 1, PANEL):
                cols[k] = cols[k] - factor * cols[k][j : j + 1, :]
            left = left - factor * left[j : j + 1, :]
            right = right - factor * right[j : j + 1, :]
            scale = jnp.where(sub == j, lax.rsqrt(jnp.broadcast_to(pivot, (PANEL, n))), scale)
        left = left * scale
        right = right * scale
        m[r0 : r0 + PANEL, 0:n] = left
        m[r0 : r0 + PANEL, n : 2 * n] = right
        r1 = r0 + PANEL
        if r1 < n:
            a, b, c = (t.astype(F32) for t in split3(jnp.concatenate([left, right], axis=1)))
            rows = jnp.concatenate([a, a, b, b, a, c], axis=0)[:, 0:n].T[r1:].astype(BF16)
            pivots = jnp.concatenate([a, b, a, b, c, a], axis=0).astype(BF16)
            m[r1:n, :] = m[r1:n, :] - dot(rows, pivots, NN)


def inverse_factor(square, m, out):
    n = HALF
    row = lax.broadcasted_iota(jnp.int32, (n, n), 0)
    col = lax.broadcasted_iota(jnp.int32, (n, n), 1)
    eye = jnp.where(row == col, 1.0, 0.0).astype(F32)
    m[:, 0:n] = square[0:n, 0:n]
    m[:, n : 2 * n] = eye
    eliminate(m)
    first = m[:, n : 2 * n]
    lower = dot(square[n:, 0:n], first, NT, HIGHEST)
    out[0:n, 0:n] = first
    out[0:n, n:] = jnp.zeros((n, n), F32)
    cross = dot(lower, first, NN, HIGHEST)
    m[:, 0:n] = square[n:, n:] - dot(lower, lower, NT, HIGHEST)
    m[:, n : 2 * n] = eye
    eliminate(m)
    second = m[:, n : 2 * n]
    out[n:, n:] = second
    out[n:, 0:n] = -dot(second, cross, NN, HIGHEST)


def kernel(
    a_ref,
    ids_ref,
    out_ref,
    vt,
    place,
    part,
    send1,
    recv1,
    chip,
    send2,
    recv2,
    low,
    full,
    acc,
    ys,
    yr,
    yg,
    sq,
    sqr1,
    sqt,
    sqr2,
    sqf,
    work,
    linv,
    outgoing,
    arrived,
    wide_f32,
    by_lane,
    s1,
    q1,
    s2,
    q2,
    s3,
    q3,
    s4,
    q4,
    ws,
    wq,
    gs,
    gq,
    es,
    eq,
    ts,
    tq,
    fs,
    fq,
):
    w = lax.axis_index("wide")
    n = lax.axis_index("narrow")
    core = lax.rem(n, 2)
    other = 1 - core
    core_peer = n + 1 - 2 * core
    chip_peer = lax.rem(n + 2, 4)

    def to(src, dst, send, recv, wide, narrow):
        return pltpu.make_async_remote_copy(
            src_ref=src,
            dst_ref=dst,
            send_sem=send,
            recv_sem=recv,
            device_id={"wide": wide, "narrow": narrow},
            device_id_type=MESH,
        )

    barrier = pltpu.get_barrier_semaphore()

    @pl.loop(1, WIDE)
    def _(i):
        pl.semaphore_signal(
            barrier, inc=1, device_id={"wide": lax.rem(w + i, WIDE), "narrow": n}, device_id_type=MESH
        )

    pl.semaphore_signal(barrier, inc=1, device_id={"wide": w, "narrow": core_peer}, device_id_type=MESH)
    pl.semaphore_signal(barrier, inc=1, device_id={"wide": w, "narrow": chip_peer}, device_id_type=MESH)

    rows = a_ref.shape[0]
    ids = ids_ref[...]
    cluster = lax.broadcasted_iota(jnp.int32, (WIDE, rows), 0)
    onehot = jnp.where(cluster == ids, 1.0, 0.0).astype(F32)
    earlier = jnp.where(
        lax.broadcasted_iota(jnp.int32, (rows, rows), 0)
        < lax.broadcasted_iota(jnp.int32, (rows, rows), 1),
        1.0,
        0.0,
    ).astype(BF16)
    counts = dot(onehot.astype(BF16), earlier, NN)
    slot = jnp.sum(counts * onehot, axis=0, keepdims=True).astype(jnp.int32)
    mine = slot - core * PIECE
    target = jnp.where((mine >= 0) & (mine < PIECE), ids * PIECE + mine, -1)

    @pl.loop(0, WIDE * PIECE, step=128)
    def _(r):
        position = lax.broadcasted_iota(jnp.int32, (128, rows), 0) + r
        place[pl.ds(r, 128), :] = jnp.where(position == target, 1.0, 0.0).astype(BF16)

    row = lax.broadcasted_iota(jnp.int32, (K, K), 0)
    col = lax.broadcasted_iota(jnp.int32, (K, K), 1)
    eye = jnp.where(row == col, 1.0, 0.0).astype(BF16)
    for g in range(CHUNKS):
        vt[:, g * K : (g + 1) * K] = eye

    pl.semaphore_wait(barrier, WIDE - 1 + 2)

    def project(it, final):
        def c1(g):
            return to(send1.at[it, g], recv1.at[it, g], s1.at[it, g], q1.at[it, g], w, core_peer)

        def c2(g):
            return to(send2.at[it, g], recv2.at[it, g], s2.at[it, g], q2.at[it, g], w, chip_peer)

        def c3(g, half):
            if final:
                block = full.at[half, g]
                return to(block, block, s4.at[g], q4.at[g], w, core_peer)
            block = low.at[it, half, g]
            return to(block, block, s3.at[it, g], q3.at[it, g], w, core_peer)

        for g in range(CHUNKS):
            now = dot(vt[...], a_ref[g * K : (g + 1) * K, :], NT)
            part[g, 0] = now[0:HALF]
            part[g, 1] = now[HALF:]
            send1[it, g] = part[g, other].astype(BF16)
            c1(g).start()
        for g in range(CHUNKS):
            c1(g).wait_recv()
            now = part[g, core] + recv1[it, g].astype(F32)
            chip[g] = now
            send2[it, g] = now.astype(BF16)
            c2(g).start()
        for g in range(CHUNKS):
            c2(g).wait_recv()
            now = chip[g] + recv2[it, g].astype(F32)
            if final:
                full[core, g] = now
            else:
                low[it, core, g] = now.astype(BF16)
            c3(g, core).start()
        return c1, c2, c3

    def sweep(it, carry):
        c1, c2, c3 = project(it, False)
        for g in range(CHUNKS):
            c3(g, other).wait_recv()
            lower = jnp.concatenate([low[it, 0, g], low[it, 1, g]], axis=0)
            for q in range(CHUNKS):
                now = dot(lower, a_ref[g * K : (g + 1) * K, q * K : (q + 1) * K], NN)
                if g > 0:
                    now = now + acc[q]
                if g < CHUNKS - 1:
                    acc[q] = now
                else:
                    ys[it, q * PIECE : (q + 1) * PIECE] = now.astype(BF16).reshape(
                        PIECE, PIECE, K
                    )

        def scatter(i):
            there = lax.rem(w + i, WIDE)
            return to(ys.at[it, there], yr.at[it, w], ws.at[it], wq.at[it], there, n)

        def gather(i):
            there = lax.rem(w + i, WIDE)
            return to(yg.at[it, w], yg.at[it, w], gs.at[it], gq.at[it], there, n)

        def drain(buffer, sem):
            block = buffer.at[it, pl.ds(0, WIDE - 1)]
            pltpu.make_async_copy(block, block, sem.at[it]).wait()

        @pl.loop(1, WIDE)
        def _(i):
            scatter(i).start()

        yr[it, w] = ys[it, w]
        for g in range(CHUNKS):
            c1(g).wait_send()
            c2(g).wait_send()
            c3(g, core).wait_send()
        drain(yr, wq)
        total = lax.fori_loop(
            0,
            WIDE,
            lambda j, t: t + yr[it, j].astype(F32),
            jnp.zeros((PIECE, K), F32),
            unroll=8,
        )
        yg[it, w] = total.astype(BF16)

        @pl.loop(1, WIDE)
        def _(i):
            gather(i).start()

        drain(ys, ws)
        drain(yg, gq)

        images = [yg[it, q * PIECE : (q + 1) * PIECE].reshape(K, K) for q in range(CHUNKS)]
        now = dot(images[0], images[0], NT)
        for q in range(1, CHUNKS):
            now = now + dot(images[q], images[q], NT)
        sq[0] = now[0:HALF]
        sq[1] = now[HALF:]

        e1 = to(sq.at[other], sqr1.at[it], es.at[it, 0], eq.at[it, 0], w, core_peer)
        e1.start()
        e1.wait_recv()
        sqt[...] = sq[core] + sqr1[it]
        e2 = to(sqt, sqr2.at[it], es.at[it, 1], eq.at[it, 1], w, chip_peer)
        e2.start()
        e2.wait_recv()
        mine = sqf.at[it, pl.ds(core * HALF, HALF)]
        mine[...] = sqt[...] + sqr2[it]
        e3 = to(mine, mine, es.at[it, 2], eq.at[it, 2], w, core_peer)
        e3.start()
        e3.wait_recv()
        inverse_factor(sqf.at[it], work, linv)
        a, b, c = split3(linv[...])
        for q in range(CHUNKS):
            y = yg[it, q * PIECE : (q + 1) * PIECE].reshape(K, K)
            vt[:, q * K : (q + 1) * K] = (
                dot(a, y, NN) + (dot(b, y, NN) + dot(c, y, NN))
            ).astype(BF16)
        e1.wait_send()
        e2.wait_send()
        e3.wait_send()
        drain(yg, gs)
        return carry

    lax.fori_loop(0, ITERS, sweep, 0)

    c1, c2, c3 = project(ITERS, True)
    for g in range(CHUNKS):
        c3(g, other).wait_recv()
        coords = jnp.concatenate([full[0, g], full[1, g]], axis=0)
        scale = lax.rsqrt(jnp.sum(coords * coords, axis=0, keepdims=True) + 1e-06)
        unit = (coords * scale).astype(BF16)
        now = dot(place[:, g * K : (g + 1) * K], unit, NT)
        if g > 0:
            now = now + wide_f32[...]
        if g < CHUNKS - 1:
            wide_f32[...] = now
        else:
            outgoing[...] = now.astype(BF16).reshape(WIDE, PIECE, K)

    def deliver(i):
        there = lax.rem(w + i, WIDE)
        return to(outgoing.at[there], arrived.at[core, w], ts, tq, there, n)

    @pl.loop(1, WIDE)
    def _(i):
        deliver(i).start()

    arrived[core, w] = outgoing[w]
    for g in range(CHUNKS):
        c1(g).wait_send()
        c2(g).wait_send()
        c3(g, core).wait_send()
    block = arrived.at[core, pl.ds(0, WIDE - 1)]
    pltpu.make_async_copy(block, block, tq).wait()
    forward = to(arrived.at[core], arrived.at[core], fs, fq, w, core_peer)
    forward.start()

    def arrange(half):
        for h in range(2):
            lanes = slice(h * HALF, (h + 1) * HALF)
            by_lane[h] = arrived[half, :, :, lanes].astype(F32).reshape(WIDE * PIECE, HALF)
            for s in range(PIECE):
                out_ref[pl.ds((half * PIECE + s) * WIDE, WIDE), lanes] = by_lane.at[h][
                    pl.ds(s, WIDE, stride=PIECE), :
                ].astype(BF16)

    arrange(core)
    to(arrived.at[other], arrived.at[other], fs, fq, w, core_peer).wait_recv()
    arrange(other)
    forward.wait_send()
    sent = outgoing.at[pl.ds(0, WIDE - 1)]
    pltpu.make_async_copy(sent, sent, ts).wait()


def members_of(embeddings, ids):
    n_it = ITERS + 1
    dma = pltpu.SemaphoreType.DMA
    vmem = pl.BlockSpec(memory_space=pltpu.VMEM)
    return pl.pallas_call(
        kernel,
        out_shape=jax.ShapeDtypeStruct((WIDE * SLOTS, K), BF16),
        in_specs=[vmem, vmem],
        out_specs=vmem,
        scratch_shapes=[
            pltpu.VMEM((K, CHUNKS * K), BF16),
            pltpu.VMEM((WIDE * PIECE, CHUNKS * K), BF16),
            pltpu.VMEM((CHUNKS, 2, HALF, K), F32),
            pltpu.VMEM((n_it, CHUNKS, HALF, K), BF16),
            pltpu.VMEM((n_it, CHUNKS, HALF, K), BF16),
            pltpu.VMEM((CHUNKS, HALF, K), F32),
            pltpu.VMEM((n_it, CHUNKS, HALF, K), BF16),
            pltpu.VMEM((n_it, CHUNKS, HALF, K), BF16),
            pltpu.VMEM((ITERS, 2, CHUNKS, HALF, K), BF16),
            pltpu.VMEM((2, CHUNKS, HALF, K), F32),
            pltpu.VMEM((CHUNKS, K, K), F32),
            pltpu.VMEM((ITERS, WIDE, PIECE, K), BF16),
            pltpu.VMEM((ITERS, WIDE, PIECE, K), BF16),
            pltpu.VMEM((ITERS, WIDE, PIECE, K), BF16),
            pltpu.VMEM((2, HALF, K), F32),
            pltpu.VMEM((ITERS, HALF, K), F32),
            pltpu.VMEM((HALF, K), F32),
            pltpu.VMEM((ITERS, HALF, K), F32),
            pltpu.VMEM((ITERS, K, K), F32),
            pltpu.VMEM((HALF, 2 * HALF), F32),
            pltpu.VMEM((K, K), F32),
            pltpu.VMEM((WIDE, PIECE, K), BF16),
            pltpu.VMEM((2, WIDE, PIECE, K), BF16),
            pltpu.VMEM((WIDE * PIECE, K), F32),
            pltpu.VMEM((2, WIDE * PIECE, HALF), F32),
            dma((n_it, CHUNKS)),
            dma((n_it, CHUNKS)),
            dma((n_it, CHUNKS)),
            dma((n_it, CHUNKS)),
            dma((ITERS, CHUNKS)),
            dma((ITERS, CHUNKS)),
            dma((CHUNKS,)),
            dma((CHUNKS,)),
            dma((ITERS,)),
            dma((ITERS,)),
            dma((ITERS,)),
            dma((ITERS,)),
            dma((ITERS, 3)),
            dma((ITERS, 3)),
            dma,
            dma,
            dma,
            dma,
        ],
        compiler_params=pltpu.CompilerParams(
            collective_id=0, has_side_effects=True, vmem_limit_bytes=48 * 1024 * 1024
        ),
        name="sketch",
    )(embeddings, ids)


def on_device(embeddings, cluster_ids):
    members = members_of(embeddings, cluster_ids.reshape(1, -1))
    count = members.shape[0] // lax.axis_size("narrow")
    own = lax.dynamic_slice_in_dim(members, lax.axis_index("narrow") * count, count, 0)
    return dot(members, own, NT).astype(BF16)[None]


def solution(mesh):
    return jax.shard_map(
        on_device,
        mesh=mesh,
        in_specs=(P("wide", "narrow"), P("wide", None)),
        out_specs=P("wide", None, "narrow"),
        check_vma=False,
    )
```

```python
import jax
import jax.numpy as jnp
from jax import lax
from jax.experimental import pallas as pl
from jax.experimental.pallas import tpu as pltpu
from jax.sharding import PartitionSpec as P

F32 = jnp.float32
BF16 = jnp.bfloat16
HIGHEST = lax.Precision.HIGHEST
MESH = pl.DeviceIdType.MESH

K = 256
ITERS = 2
HALF = 128
PANEL = 16
CHUNKS = 4
WIDE = 64
PIECE = 16
SLOTS = 32
RING = 4
PLANE = 16


def dot(a, b, dims, precision=None):
    return lax.dot_general(
        a, b, (dims, ((), ())), precision=precision, preferred_element_type=F32
    )


NN = ((1,), (0,))
NT = ((1,), (1,))


def split2(x):
    a = x.astype(BF16)
    return a, (x - a.astype(F32)).astype(BF16)


def split3(x):
    a = x.astype(BF16)
    b, c = split2(x - a.astype(F32))
    return a, b, c


def eliminate(m):
    n = HALF
    sub = lax.broadcasted_iota(jnp.int32, (PANEL, n), 0)
    for r0 in range(0, n, PANEL):
        left = m[r0 : r0 + PANEL, 0:n]
        right = m[r0 : r0 + PANEL, n : 2 * n]
        cols = [
            jnp.broadcast_to(left[:, r0 + j : r0 + j + 1], (PANEL, n)) for j in range(PANEL)
        ]
        scale = jnp.zeros((PANEL, n), F32)
        for j in range(PANEL):
            pivot = cols[j][j : j + 1, :]
            factor = jnp.where(sub > j, cols[j] * (1.0 / pivot), 0.0)
            for k in range(j + 1, PANEL):
                cols[k] = cols[k] - factor * cols[k][j : j + 1, :]
            left = left - factor * left[j : j + 1, :]
            right = right - factor * right[j : j + 1, :]
            scale = jnp.where(sub == j, lax.rsqrt(jnp.broadcast_to(pivot, (PANEL, n))), scale)
        left = left * scale
        right = right * scale
        m[r0 : r0 + PANEL, 0:n] = left
        m[r0 : r0 + PANEL, n : 2 * n] = right
        r1 = r0 + PANEL
        if r1 < n:
            a, b, c = (t.astype(F32) for t in split3(jnp.concatenate([left, right], axis=1)))
            rows = jnp.concatenate([a, a, b, b, a, c], axis=0)[:, 0:n].T[r1:].astype(BF16)
            pivots = jnp.concatenate([a, b, a, b, c, a], axis=0).astype(BF16)
            m[r1:n, :] = m[r1:n, :] - dot(rows, pivots, NN)


def inverse_factor_start(square, m, out, cross):
    n = HALF
    row = lax.broadcasted_iota(jnp.int32, (n, n), 0)
    col = lax.broadcasted_iota(jnp.int32, (n, n), 1)
    eye = jnp.where(row == col, 1.0, 0.0).astype(F32)
    m[:, 0:n] = square[0:n, 0:n]
    m[:, n : 2 * n] = eye
    eliminate(m)
    first = m[:, n : 2 * n]
    lower = dot(square[n:, 0:n], first, NT, HIGHEST)
    out[0:n, 0:n] = first
    out[0:n, n:] = jnp.zeros((n, n), F32)
    cross[...] = dot(lower, first, NN, HIGHEST)
    m[:, 0:n] = square[n:, n:] - dot(lower, lower, NT, HIGHEST)
    m[:, n : 2 * n] = eye


def inverse_factor_end(m, out, cross):
    n = HALF
    eliminate(m)
    second = m[:, n : 2 * n]
    out[n:, n:] = second
    out[n:, 0:n] = -dot(second, cross[...], NN, HIGHEST)


def kernel(
    a_hbm,
    ids_ref,
    out_ref,
    a_ref,
    vt,
    place,
    part,
    recv1,
    chip,
    send2,
    recv2,
    full,
    coords,
    low,
    ys,
    yr1,
    own,
    ysb,
    yr2,
    mine4,
    yg,
    sq,
    sqr1,
    sqt,
    sqr2,
    sqf,
    work,
    cross,
    linv,
    outgoing,
    arrived,
    by_lane,
    load_sem,
    s1,
    q1,
    s2,
    q2,
    s3,
    q3,
    as_,
    aq,
    bs,
    bq,
    cs,
    cq,
    ds,
    dq,
    es,
    eq,
    ts,
    tq,
    fs,
    fq,
):
    w = lax.axis_index("wide")
    n = lax.axis_index("narrow")
    core = lax.rem(n, 2)
    other = 1 - core
    core_peer = n + 1 - 2 * core
    chip_peer = lax.rem(n + 2, 4)
    z = w // 8
    y = lax.rem(w // 2, RING)
    x = lax.rem(w, 2)
    plane = z * 2 + x
    quad = z // 2
    within = lax.rem(plane, RING)

    def at(there, ring):
        return (there // 2) * 8 + ring * 2 + lax.rem(there, 2)

    def to(src, dst, send, recv, wide, narrow):
        return pltpu.make_async_remote_copy(
            src_ref=src,
            dst_ref=dst,
            send_sem=send,
            recv_sem=recv,
            device_id={"wide": wide, "narrow": narrow},
            device_id_type=MESH,
        )

    def settle(block, sem):
        pltpu.make_async_copy(block, block, sem).wait()

    def load(g):
        piece = pl.ds(g * K, K)
        return pltpu.make_async_copy(a_hbm.at[piece], a_ref.at[piece], load_sem.at[g])

    for g in range(CHUNKS):
        load(g).start()

    barrier = pltpu.get_barrier_semaphore()

    @pl.loop(1, WIDE)
    def _(i):
        pl.semaphore_signal(
            barrier,
            inc=1,
            device_id={"wide": lax.rem(w + i, WIDE), "narrow": n},
            device_id_type=MESH,
        )

    for peer in (core_peer, chip_peer):
        pl.semaphore_signal(
            barrier, inc=1, device_id={"wide": w, "narrow": peer}, device_id_type=MESH
        )

    row = lax.broadcasted_iota(jnp.int32, (K, K), 0)
    col = lax.broadcasted_iota(jnp.int32, (K, K), 1)
    eye = jnp.where(row == col, 1.0, 0.0).astype(BF16)
    for g in range(CHUNKS):
        vt[:, g * K : (g + 1) * K] = eye

    def c1(it, g):
        return to(part.at[g, other], recv1.at[it, g], s1.at[it, g], q1.at[it, g], w, core_peer)

    def c2(it, g):
        return to(send2.at[it, g], recv2.at[it, g], s2.at[it, g], q2.at[it, g], w, chip_peer)

    def c3(it, g, half):
        block = full.at[it, g, half]
        return to(block, block, s3.at[it, g], q3.at[it, g], w, core_peer)

    def project(g):
        now = dot(vt[...], a_ref[g * K : (g + 1) * K, :], NT)
        part[g, 0] = now[0:HALF]
        part[g, 1] = now[HALF:]

    def over_cores(it, g):
        c1(it, g).wait_recv()
        now = part[g, core] + recv1[it, g]
        chip[g] = now
        send2[it, g] = now.astype(BF16)
        c2(it, g).start()

    def over_chips(it, g):
        c2(it, g).wait_recv()
        full[it, g, core] = chip[g] + recv2[it, g].astype(F32)
        c3(it, g, core).start()

    def whole(it, g):
        c3(it, g, other).wait_recv()
        return jnp.concatenate([full[it, g, 0], full[it, g, 1]], axis=0)

    def sent(it):
        for g in range(CHUNKS):
            c1(it, g).wait_send()
            c2(it, g).wait_send()
            c3(it, g, core).wait_send()

    for g in range(CHUNKS):
        load(g).wait()
        project(g)
        if g == 0:
            pl.semaphore_wait(barrier, WIDE - 1 + 2)
        c1(0, g).start()
    for g in range(CHUNKS):
        over_cores(0, g)

    rows = a_ref.shape[0]
    ids = ids_ref[...]
    cluster = lax.broadcasted_iota(jnp.int32, (WIDE, rows), 0)
    onehot = jnp.where(cluster == ids, 1.0, 0.0).astype(F32)
    earlier = jnp.where(
        lax.broadcasted_iota(jnp.int32, (rows, rows), 0)
        < lax.broadcasted_iota(jnp.int32, (rows, rows), 1),
        1.0,
        0.0,
    ).astype(BF16)
    counts = dot(onehot.astype(BF16), earlier, NN)
    slot = jnp.sum(counts * onehot, axis=0, keepdims=True).astype(jnp.int32)
    offset = slot - core * PIECE
    target = jnp.where((offset >= 0) & (offset < PIECE), ids * PIECE + offset, -1)

    @pl.loop(0, WIDE * PIECE, step=128)
    def _(r):
        position = lax.broadcasted_iota(jnp.int32, (128, rows), 0) + r
        place[pl.ds(r, 128), :] = jnp.where(position == target, 1.0, 0.0).astype(BF16)

    for g in range(CHUNKS):
        over_chips(0, g)
    for g in range(CHUNKS):
        low[:, g * K : (g + 1) * K] = whole(0, g).astype(BF16)
    sent(0)

    def sweep(it, carry):
        def first(off, c, k):
            piece = pl.ds(c * RING, RING)
            return to(
                ys.at[it, off - 1, piece],
                yr1.at[it, off - 1, piece],
                as_.at[it],
                aq.at[it, k],
                at(plane, lax.rem(y + off, RING)),
                n,
            )

        order = (2, 1, 3, 0)
        for off in order:
            q = lax.rem(y + off, RING)
            now = dot(low[...], a_ref[:, pl.ds(pl.multiple_of(q * K, K), K)], NN)
            if off:
                ys[it, off - 1] = now.astype(BF16).reshape(PLANE, PIECE, K)
                for k, turn in enumerate(order):
                    first(off, lax.rem(quad + turn, RING), k).start()
            else:
                own[...] = now.reshape(PLANE, PIECE, K)

        for k, turn in enumerate(order):
            c = lax.rem(quad + turn, RING)
            settle(yr1.at[it, :, pl.ds(0, RING)], aq.at[it, k])
            piece = pl.ds(c * RING, RING)
            now = own[piece]
            for off in (1, 2, 3):
                now = now + yr1[it, off - 1, piece].astype(F32)
            ysb[it, piece] = now.astype(BF16)
            if turn == 0:
                mine4[...] = now
            for t in range(0 if turn else 1, RING):
                there = c * RING + lax.rem(within + t, RING)
                to(ysb.at[it, there], yr2.at[it, plane], bs.at[it], bq.at[it], at(there, y), n).start()
        settle(yr2.at[it, pl.ds(0, PLANE - 1)], bq.at[it])
        total = mine4[within]
        for t in range(1, PLANE):
            total = total + yr2[it, lax.rem(plane + t, PLANE)].astype(F32)
        mine = yg.at[it, y * PLANE + plane]
        mine[...] = total.astype(BF16)

        @pl.loop(1, PLANE)
        def _(t):
            there = lax.rem(plane + t, PLANE)
            block = yg.at[it, y * PLANE + plane]
            to(block, block, cs.at[it], cq.at[it, quad], at(there, y), n).start()

        for turn in (0, 1, 3, 2):
            c = lax.rem(quad + turn, RING)
            settle(yg.at[it, pl.ds(0, RING if turn else RING - 1)], cq.at[it, c])
            block = yg.at[it, pl.ds(y * PLANE + c * RING, RING)]
            for off in (2, 1, 3):
                ring = lax.rem(y + off, RING)
                to(block, block, ds.at[it], dq.at[it, off - 1], at(plane, ring), n).start()
        for off in (0, 1, 3, 2):
            q = lax.rem(y - off + RING, RING)
            if off:
                settle(yg.at[it, pl.ds(0, PLANE)], dq.at[it, off - 1])
            vt[:, pl.ds(pl.multiple_of(q * K, K), K)] = yg[it, pl.ds(q * PLANE, PLANE)].reshape(K, K)

        now = dot(vt[...], vt[...], NT)
        sq[0] = now[0:HALF]
        sq[1] = now[HALF:]
        e1 = to(sq.at[other], sqr1.at[it], es.at[it, 0], eq.at[it, 0], w, core_peer)
        e1.start()
        later = it + 1
        for g in range(CHUNKS):
            project(g)
            c1(later, g).start()
        e1.wait_recv()
        sqt[...] = sq[core] + sqr1[it]
        e2 = to(sqt, sqr2.at[it], es.at[it, 1], eq.at[it, 1], w, chip_peer)
        e2.start()
        for g in range(CHUNKS):
            over_cores(later, g)
        e2.wait_recv()
        half = sqf.at[it, pl.ds(core * HALF, HALF)]
        half[...] = sqt[...] + sqr2[it]
        e3 = to(half, half, es.at[it, 2], eq.at[it, 2], w, core_peer)
        e3.start()
        rest = sqf.at[it, pl.ds(other * HALF, HALF)]
        to(rest, rest, es.at[it, 2], eq.at[it, 2], w, core_peer).wait_recv()
        inverse_factor_start(sqf.at[it], work, linv, cross)
        for g in range(CHUNKS):
            over_chips(later, g)
        inverse_factor_end(work, linv, cross)
        a, b = split2(linv[...])
        for g in range(CHUNKS):
            c, d = split2(whole(later, g))
            now = dot(a, c, NN) + (dot(a, d, NN) + dot(b, c, NN))
            coords[g] = now
            low[:, g * K : (g + 1) * K] = now.astype(BF16)

        sent(later)
        e1.wait_send()
        e2.wait_send()
        e3.wait_send()
        settle(ys.at[it], as_.at[it])
        settle(ysb.at[it, pl.ds(0, PLANE - 1)], bs.at[it])
        settle(yg.at[it, pl.ds(0, PLANE - 1)], cs.at[it])
        settle(ys.at[it], ds.at[it])
        return carry

    lax.fori_loop(0, ITERS, sweep, 0)

    for g in range(CHUNKS):
        now = coords[g]
        scale = lax.rsqrt(jnp.sum(now * now, axis=0, keepdims=True) + 1e-06)
        low[:, g * K : (g + 1) * K] = (now * scale).astype(BF16)
    outgoing[...] = dot(place[...], low[...], NT).astype(BF16).reshape(WIDE, PIECE, K)

    @pl.loop(1, WIDE)
    def _(i):
        there = lax.rem(w + i, WIDE)
        to(outgoing.at[there], arrived.at[core, w], ts, tq, there, n).start()

    arrived[core, w] = outgoing[w]
    settle(arrived.at[core, pl.ds(0, WIDE - 1)], tq)
    forward = to(arrived.at[core], arrived.at[core], fs, fq, w, core_peer)
    forward.start()

    def arrange(half):
        for h in range(2):
            lanes = slice(h * HALF, (h + 1) * HALF)
            by_lane[h] = arrived[half, :, :, lanes].astype(F32).reshape(WIDE * PIECE, HALF)
            for s in range(PIECE):
                out_ref[pl.ds((half * PIECE + s) * WIDE, WIDE), lanes] = by_lane.at[h][
                    pl.ds(s, WIDE, stride=PIECE), :
                ].astype(BF16)

    arrange(core)
    to(arrived.at[other], arrived.at[other], fs, fq, w, core_peer).wait_recv()
    arrange(other)
    forward.wait_send()
    settle(outgoing.at[pl.ds(0, WIDE - 1)], ts)


def members_of(embeddings, ids):
    n_it = ITERS + 1
    dma = pltpu.SemaphoreType.DMA
    vmem = pl.BlockSpec(memory_space=pltpu.VMEM)
    return pl.pallas_call(
        kernel,
        out_shape=jax.ShapeDtypeStruct((WIDE * SLOTS, K), BF16),
        in_specs=[pl.BlockSpec(memory_space=pl.ANY), vmem],
        out_specs=vmem,
        scratch_shapes=[
            pltpu.VMEM((CHUNKS * K, CHUNKS * K), BF16),
            pltpu.VMEM((K, CHUNKS * K), BF16),
            pltpu.VMEM((WIDE * PIECE, CHUNKS * K), BF16),
            pltpu.VMEM((CHUNKS, 2, HALF, K), F32),
            pltpu.VMEM((n_it, CHUNKS, HALF, K), F32),
            pltpu.VMEM((CHUNKS, HALF, K), F32),
            pltpu.VMEM((n_it, CHUNKS, HALF, K), BF16),
            pltpu.VMEM((n_it, CHUNKS, HALF, K), BF16),
            pltpu.VMEM((n_it, CHUNKS, 2, HALF, K), F32),
            pltpu.VMEM((CHUNKS, K, K), F32),
            pltpu.VMEM((K, CHUNKS * K), BF16),
            pltpu.VMEM((ITERS, RING - 1, PLANE, PIECE, K), BF16),
            pltpu.VMEM((ITERS, RING - 1, PLANE, PIECE, K), BF16),
            pltpu.VMEM((PLANE, PIECE, K), F32),
            pltpu.VMEM((ITERS, PLANE, PIECE, K), BF16),
            pltpu.VMEM((ITERS, PLANE, PIECE, K), BF16),
            pltpu.VMEM((RING, PIECE, K), F32),
            pltpu.VMEM((ITERS, WIDE, PIECE, K), BF16),
            pltpu.VMEM((2, HALF, K), F32),
            pltpu.VMEM((ITERS, HALF, K), F32),
            pltpu.VMEM((HALF, K), F32),
            pltpu.VMEM((ITERS, HALF, K), F32),
            pltpu.VMEM((ITERS, K, K), F32),
            pltpu.VMEM((HALF, 2 * HALF), F32),
            pltpu.VMEM((HALF, HALF), F32),
            pltpu.VMEM((K, K), F32),
            pltpu.VMEM((WIDE, PIECE, K), BF16),
            pltpu.VMEM((2, WIDE, PIECE, K), BF16),
            pltpu.VMEM((2, WIDE * PIECE, HALF), F32),
            dma((CHUNKS,)),
            *[dma((n_it, CHUNKS))] * 6,
            dma((ITERS,)),
            dma((ITERS, RING)),
            dma((ITERS,)),
            dma((ITERS,)),
            dma((ITERS,)),
            dma((ITERS, RING)),
            dma((ITERS,)),
            dma((ITERS, RING - 1)),
            dma((ITERS, 3)),
            dma((ITERS, 3)),
            dma,
            dma,
            dma,
            dma,
        ],
        compiler_params=pltpu.CompilerParams(
            collective_id=0, has_side_effects=True, vmem_limit_bytes=56 * 1024 * 1024
        ),
        name="sketch",
    )(embeddings, ids)


def on_device(embeddings, cluster_ids):
    members = members_of(embeddings, cluster_ids.reshape(1, -1))
    count = members.shape[0] // lax.axis_size("narrow")
    own = lax.dynamic_slice_in_dim(members, lax.axis_index("narrow") * count, count, 0)
    return dot(members, own, NT).astype(BF16)[None]


def solution(mesh):
    return jax.shard_map(
        on_device,
        mesh=mesh,
        in_specs=(P("wide", "narrow"), P("wide", None)),
        out_specs=P("wide", None, "narrow"),
        check_vma=False,
    )
```

```python
import jax
import jax.numpy as jnp
from jax import lax
from jax.experimental import pallas as pl
from jax.experimental.pallas import tpu as pltpu
from jax.sharding import PartitionSpec as P

F32 = jnp.float32
BF16 = jnp.bfloat16
HIGHEST = lax.Precision.HIGHEST
MESH = pl.DeviceIdType.MESH

K = 256
ITERS = 2
HALF = 128
PANEL = 16
CHUNKS = 4
WIDE = 64
PIECE = 16
SLOTS = 32
RING = 4
PLANE = 16
QUARTER = 8


def dot(a, b, dims, precision=None):
    return lax.dot_general(
        a, b, (dims, ((), ())), precision=precision, preferred_element_type=F32
    )


NN = ((1,), (0,))
NT = ((1,), (1,))


def split2(x):
    a = x.astype(BF16)
    return a, (x - a.astype(F32)).astype(BF16)


def split3(x):
    a = x.astype(BF16)
    b, c = split2(x - a.astype(F32))
    return a, b, c


def eliminate(m, between=None):
    n = HALF
    sub = lax.broadcasted_iota(jnp.int32, (PANEL, n), 0)
    for r0 in range(0, n, PANEL):
        left = m[r0 : r0 + PANEL, 0:n]
        right = m[r0 : r0 + PANEL, n : 2 * n]
        cols = [
            jnp.broadcast_to(left[:, r0 + j : r0 + j + 1], (PANEL, n)) for j in range(PANEL)
        ]
        scale = jnp.zeros((PANEL, n), F32)
        for j in range(PANEL):
            pivot = cols[j][j : j + 1, :]
            factor = jnp.where(sub > j, cols[j] * (1.0 / pivot), 0.0)
            for k in range(j + 1, PANEL):
                cols[k] = cols[k] - factor * cols[k][j : j + 1, :]
            left = left - factor * left[j : j + 1, :]
            right = right - factor * right[j : j + 1, :]
            scale = jnp.where(sub == j, lax.rsqrt(jnp.broadcast_to(pivot, (PANEL, n))), scale)
        left = left * scale
        right = right * scale
        m[r0 : r0 + PANEL, 0:n] = left
        m[r0 : r0 + PANEL, n : 2 * n] = right
        r1 = r0 + PANEL
        if r1 < n:
            a, b, c = (t.astype(F32) for t in split3(jnp.concatenate([left, right], axis=1)))
            rows = jnp.concatenate([a, a, b, b, a, c], axis=0)[:, 0:n].T[r1:].astype(BF16)
            pivots = jnp.concatenate([a, b, a, b, c, a], axis=0).astype(BF16)
            m[r1:n, :] = m[r1:n, :] - dot(rows, pivots, NN)
        if between is not None:
            between(r0 // PANEL)


def inverse_factor_start(square, m, out, cross):
    n = HALF
    row = lax.broadcasted_iota(jnp.int32, (n, n), 0)
    col = lax.broadcasted_iota(jnp.int32, (n, n), 1)
    eye = jnp.where(row == col, 1.0, 0.0).astype(F32)
    m[:, 0:n] = square[0:n, 0:n]
    m[:, n : 2 * n] = eye
    eliminate(m)
    first = m[:, n : 2 * n]
    lower = dot(square[n:, 0:n], first, NT, HIGHEST)
    out[0:n, 0:n] = first
    out[0:n, n:] = jnp.zeros((n, n), F32)
    cross[...] = dot(lower, first, NN, HIGHEST)
    m[:, 0:n] = square[n:, n:] - dot(lower, lower, NT, HIGHEST)
    m[:, n : 2 * n] = eye


def inverse_factor_end(m, out, cross, between):
    n = HALF
    eliminate(m, between)
    second = m[:, n : 2 * n]
    out[n:, n:] = second
    out[n:, 0:n] = -dot(second, cross[...], NN, HIGHEST)


def to(src, dst, send, recv, wide, narrow):
    return pltpu.make_async_remote_copy(
        src_ref=src,
        dst_ref=dst,
        send_sem=send,
        recv_sem=recv,
        device_id={"wide": wide, "narrow": narrow},
        device_id_type=MESH,
    )


def settle(block, sem):
    pltpu.make_async_copy(block, block, sem).wait()


def signal(barrier, wide, narrow):
    pl.semaphore_signal(
        barrier, inc=1, device_id={"wide": wide, "narrow": narrow}, device_id_type=MESH
    )


def sum_over_narrow(w, n, vt, a_ref, part, recv1, chip, send2, recv2, full, sems):
    core = lax.rem(n, 2)
    other = 1 - core
    core_peer = n + 1 - 2 * core
    chip_peer = lax.rem(n + 2, 4)
    s1, q1, s2, q2, s3, q3 = sems

    def c1(it, g):
        return to(part.at[g, other], recv1.at[it, g], s1.at[it, g], q1.at[it, g], w, core_peer)

    def c2(it, g):
        return to(send2.at[it, g], recv2.at[it, g], s2.at[it, g], q2.at[it, g], w, chip_peer)

    def c3(it, g, half):
        block = full.at[it, g, half]
        return to(block, block, s3.at[it, g], q3.at[it, g], w, core_peer)

    def project(it, g):
        now = dot(vt[...], a_ref[g * K : (g + 1) * K, :], NT)
        part[g, 0] = now[0:HALF]
        part[g, 1] = now[HALF:]
        c1(it, g).start()

    def over_cores(it, g):
        c1(it, g).wait_recv()
        now = part[g, core] + recv1[it, g]
        chip[g] = now
        send2[it, g] = now.astype(BF16)
        c2(it, g).start()

    def over_chips(it, g):
        c2(it, g).wait_recv()
        full[it, g, core] = chip[g] + recv2[it, g].astype(F32)
        c3(it, g, core).start()

    def whole(it, g):
        c3(it, g, other).wait_recv()
        return jnp.concatenate([full[it, g, 0], full[it, g, 1]], axis=0)

    def sent(it):
        for g in range(CHUNKS):
            c1(it, g).wait_send()
            c2(it, g).wait_send()
            c3(it, g, core).wait_send()

    return project, over_cores, over_chips, whole, sent


def first_kernel(
    a_hbm,
    ids_ref,
    a_ref,
    low_ref,
    place,
    vt,
    part,
    recv1,
    chip,
    send2,
    recv2,
    full,
    load_sem,
    s1,
    q1,
    s2,
    q2,
    s3,
    q3,
):
    w = lax.axis_index("wide")
    n = lax.axis_index("narrow")
    barrier = pltpu.get_barrier_semaphore()
    signal(barrier, w, n + 1 - 2 * lax.rem(n, 2))
    signal(barrier, w, lax.rem(n + 2, 4))

    def load(g):
        piece = pl.ds(g * K, K)
        return pltpu.make_async_copy(a_hbm.at[piece], a_ref.at[piece], load_sem.at[g])

    for g in range(CHUNKS):
        load(g).start()
    row = lax.broadcasted_iota(jnp.int32, (K, K), 0)
    col = lax.broadcasted_iota(jnp.int32, (K, K), 1)
    eye = jnp.where(row == col, 1.0, 0.0).astype(BF16)
    for g in range(CHUNKS):
        vt[:, g * K : (g + 1) * K] = eye
    project, over_cores, over_chips, whole, sent = sum_over_narrow(
        w, n, vt, a_ref, part, recv1, chip, send2, recv2, full, (s1, q1, s2, q2, s3, q3)
    )
    pl.semaphore_wait(barrier, 2)
    for g in range(CHUNKS):
        load(g).wait()
        project(0, g)
    for g in range(CHUNKS):
        over_cores(0, g)
    rows = a_ref.shape[0]
    ids = ids_ref[...]
    cluster = lax.broadcasted_iota(jnp.int32, (WIDE, rows), 0)
    onehot = jnp.where(cluster == ids, 1.0, 0.0).astype(F32)
    earlier = jnp.where(
        lax.broadcasted_iota(jnp.int32, (rows, rows), 0)
        < lax.broadcasted_iota(jnp.int32, (rows, rows), 1),
        1.0,
        0.0,
    ).astype(BF16)
    counts = dot(onehot.astype(BF16), earlier, NN)
    slot = jnp.sum(counts * onehot, axis=0, keepdims=True).astype(jnp.int32)
    offset = slot - n * QUARTER
    owner = ((ids >> 1) & 3) * PLANE + (ids >> 3) * 2 + (ids & 1)
    target = jnp.where((offset >= 0) & (offset < QUARTER), owner * QUARTER + offset, -1)

    @pl.loop(0, WIDE * QUARTER, step=128)
    def _(r):
        position = lax.broadcasted_iota(jnp.int32, (128, rows), 0) + r
        place[pl.ds(r, 128), :] = jnp.where(position == target, 1.0, 0.0).astype(BF16)
    for g in range(CHUNKS):
        over_chips(0, g)
    for g in range(CHUNKS):
        low_ref[:, g * K : (g + 1) * K] = whole(0, g).astype(BF16)
    sent(0)


def kernel(
    a_ref,
    low_ref,
    place,
    out_ref,
    vt,
    part,
    recv1,
    chip,
    send2,
    recv2,
    full,
    coords,
    low,
    ys,
    yr1,
    own,
    ysb,
    yr2,
    mine4,
    yg,
    sq,
    sqr1,
    sqt,
    sqr2,
    sqf,
    work,
    cross,
    linv,
    outgoing,
    arrived,
    by_lane,
    s1,
    q1,
    s2,
    q2,
    s3,
    q3,
    as_,
    aq,
    bs,
    bq,
    cs,
    cq,
    ds,
    dq,
    es,
    eq,
    ts,
    tq,
    vs,
    vq,
    fs,
    fq,
    gs,
):
    w = lax.axis_index("wide")
    n = lax.axis_index("narrow")
    core = lax.rem(n, 2)
    other = 1 - core
    core_peer = n + 1 - 2 * core
    chip_peer = lax.rem(n + 2, 4)
    z = w // 8
    y = lax.rem(w // 2, RING)
    x = lax.rem(w, 2)
    plane = z * 2 + x
    quad = z // 2
    within = lax.rem(plane, RING)

    def at(there, ring):
        return (there // 2) * 8 + ring * 2 + lax.rem(there, 2)

    barrier = pltpu.get_barrier_semaphore()

    @pl.loop(1, PLANE)
    def _(t):
        signal(barrier, at(lax.rem(plane + t, PLANE), y), n)

    for off in range(1, RING):
        signal(barrier, at(plane, lax.rem(y + off, RING)), n)
    signal(barrier, w, core_peer)
    signal(barrier, w, chip_peer)
    project, over_cores, over_chips, whole, sent = sum_over_narrow(
        w, n, vt, a_ref, part, recv1, chip, send2, recv2, full, (s1, q1, s2, q2, s3, q3)
    )
    low[...] = low_ref[...]
    pl.semaphore_wait(barrier, PLANE - 1 + RING - 1 + 2)

    def sweep(it, carry):
        def first(off, c, k):
            piece = pl.ds(c * RING, RING)
            return to(
                ys.at[it, off - 1, piece],
                yr1.at[it, off - 1, piece],
                as_.at[it],
                aq.at[it, k],
                at(plane, lax.rem(y + off, RING)),
                n,
            )

        order = (2, 1, 3, 0)
        for off in order:
            q = lax.rem(y + off, RING)
            now = dot(low[...], a_ref[:, pl.ds(pl.multiple_of(q * K, K), K)], NN)
            if off:
                ys[it, off - 1] = now.astype(BF16).reshape(PLANE, PIECE, K)
            else:
                own[...] = now.reshape(PLANE, PIECE, K)
            if off == 3:
                for k, turn in enumerate(order):
                    for there in (2, 1, 3):
                        first(there, lax.rem(quad + turn, RING), k).start()

        for k, turn in enumerate(order):
            c = lax.rem(quad + turn, RING)
            settle(yr1.at[it, :, pl.ds(0, RING)], aq.at[it, k])
            piece = pl.ds(c * RING, RING)
            now = own[piece]
            for off in (1, 2, 3):
                now = now + yr1[it, off - 1, piece].astype(F32)
            ysb[it, piece] = now.astype(BF16)
            if turn == 0:
                mine4[...] = now
            for t in range(0 if turn else 1, RING):
                there = c * RING + lax.rem(within + t, RING)
                to(ysb.at[it, there], yr2.at[it, plane], bs.at[it], bq.at[it], at(there, y), n).start()
        settle(yr2.at[it, pl.ds(0, PLANE - 1)], bq.at[it])
        total = mine4[within]
        for t in range(1, PLANE):
            total = total + yr2[it, lax.rem(plane + t, PLANE)].astype(F32)
        mine = yg.at[it, y * PLANE + plane]
        mine[...] = total.astype(BF16)

        @pl.loop(1, PLANE)
        def _(t):
            there = lax.rem(plane + t, PLANE)
            block = yg.at[it, y * PLANE + plane]
            to(block, block, cs.at[it], cq.at[it, quad], at(there, y), n).start()

        for turn in (0, 1, 3, 2):
            c = lax.rem(quad + turn, RING)
            settle(yg.at[it, pl.ds(0, RING if turn else RING - 1)], cq.at[it, c])
            block = yg.at[it, pl.ds(y * PLANE + c * RING, RING)]
            for off in (2, 1, 3):
                ring = lax.rem(y + off, RING)
                to(block, block, ds.at[it], dq.at[it, off - 1], at(plane, ring), n).start()
        for off in (0, 1, 3, 2):
            q = lax.rem(y - off + RING, RING)
            if off:
                settle(yg.at[it, pl.ds(0, PLANE)], dq.at[it, off - 1])
            vt[:, pl.ds(pl.multiple_of(q * K, K), K)] = yg[it, pl.ds(q * PLANE, PLANE)].reshape(K, K)

        now = dot(vt[...], vt[...], NT)
        sq[0] = now[0:HALF]
        sq[1] = now[HALF:]
        e1 = to(sq.at[other], sqr1.at[it], es.at[it, 0], eq.at[it, 0], w, core_peer)
        e1.start()
        for g in range(CHUNKS):
            project(it, g)
        e1.wait_recv()
        sqt[...] = sq[core] + sqr1[it]
        e2 = to(sqt, sqr2.at[it], es.at[it, 1], eq.at[it, 1], w, chip_peer)
        e2.start()
        e2.wait_recv()
        half = sqf.at[it, pl.ds(core * HALF, HALF)]
        half[...] = sqt[...] + sqr2[it]
        e3 = to(half, half, es.at[it, 2], eq.at[it, 2], w, core_peer)
        e3.start()
        for g in range(CHUNKS):
            over_cores(it, g)
        rest = sqf.at[it, pl.ds(other * HALF, HALF)]
        to(rest, rest, es.at[it, 2], eq.at[it, 2], w, core_peer).wait_recv()
        inverse_factor_start(sqf.at[it], work, linv, cross)


        def between(panel):
            if panel in (3, 4, 5, 6):
                over_chips(it, panel - 3)

        inverse_factor_end(work, linv, cross, between)
        a, b = split2(linv[...])
        for g in range(CHUNKS):
            c, d = split2(whole(it, g))
            now = dot(a, c, NN) + (dot(a, d, NN) + dot(b, c, NN))
            coords[g] = now
            low[:, g * K : (g + 1) * K] = now.astype(BF16)

        sent(it)
        e1.wait_send()
        e2.wait_send()
        e3.wait_send()
        settle(ys.at[it], as_.at[it])
        settle(ysb.at[it, pl.ds(0, PLANE - 1)], bs.at[it])
        settle(yg.at[it, pl.ds(0, PLANE - 1)], cs.at[it])
        settle(ys.at[it], ds.at[it])
        return carry

    lax.fori_loop(0, ITERS, sweep, 0)

    for g in range(CHUNKS):
        now = coords[g]
        scale = lax.rsqrt(jnp.sum(now * now, axis=0, keepdims=True) + 1e-06)
        low[:, g * K : (g + 1) * K] = (now * scale).astype(BF16)
    now = dot(place[...], low[...], NT).reshape(RING, PLANE, QUARTER, K)
    outgoing[...] = jnp.concatenate([now[..., 0:HALF], now[..., HALF:]], axis=2).astype(BF16)

    for turn in (0, 1, 3, 2):
        c = lax.rem(quad + turn, RING)

        @pl.loop(0, PLANE)
        def _(t):
            ring = lax.rem(y + t, RING)
            there = c * RING + lax.rem(within + t // RING, RING)

            def send():
                to(
                    outgoing.at[ring, there],
                    arrived.at[n, z, y, x],
                    ts,
                    tq.at[quad],
                    at(there, ring),
                    n,
                ).start()

            if turn == 0:
                pl.when(t > 0)(send)
            else:
                send()

    arrived[n, z, y, x] = outgoing[y, plane]

    def share(c, who, peer, send, recv):
        block = arrived.at[who, pl.ds(c * 2, 2)]
        return to(block, block, send, recv, w, peer)

    for turn in (0, 1, 3, 2):
        c = lax.rem(quad + turn, RING)
        count = PLANE if turn else PLANE - 1
        settle(outgoing.at[0, pl.ds(0, count)], tq.at[c])
        share(c, n, chip_peer, vs, vq.at[c]).start()
        share(c, n, core_peer, fs, fq.at[0]).start()

    def arrange(who):
        by_lane[...] = arrived[who].astype(F32).reshape(WIDE * PIECE, HALF)
        for h in range(2):
            for s in range(QUARTER):
                out_ref[
                    pl.ds((who * QUARTER + s) * WIDE, WIDE), h * HALF : (h + 1) * HALF
                ] = by_lane[pl.ds(h * QUARTER + s, WIDE, stride=PIECE), :].astype(BF16)

    arrange(n)
    for turn in (0, 1, 3, 2):
        c = lax.rem(quad + turn, RING)
        share(c, chip_peer, chip_peer, vs, vq.at[c]).wait_recv()
        share(c, chip_peer, core_peer, gs, fq.at[1]).start()
    settle(arrived.at[core_peer], fq.at[0])
    arrange(core_peer)
    arrange(chip_peer)
    last = lax.rem(core_peer + 2, 4)
    settle(arrived.at[last], fq.at[1])
    arrange(last)
    settle(arrived.at[n], fs)
    settle(arrived.at[n], vs)
    settle(arrived.at[n], gs)
    for _ in range(RING - 1):
        settle(outgoing.at[0], ts)
    settle(outgoing.at[0, pl.ds(0, PLANE - 1)], ts)


def members_of(embeddings, ids):
    dma = pltpu.SemaphoreType.DMA
    vmem = pl.BlockSpec(memory_space=pltpu.VMEM)

    def narrow_scratch(times):
        return [
            pltpu.VMEM((K, CHUNKS * K), BF16),
            pltpu.VMEM((CHUNKS, 2, HALF, K), F32),
            pltpu.VMEM((times, CHUNKS, HALF, K), F32),
            pltpu.VMEM((CHUNKS, HALF, K), F32),
            pltpu.VMEM((times, CHUNKS, HALF, K), BF16),
            pltpu.VMEM((times, CHUNKS, HALF, K), BF16),
            pltpu.VMEM((times, CHUNKS, 2, HALF, K), F32),
        ]

    a, low, place = pl.pallas_call(
        first_kernel,
        out_shape=[
            jax.ShapeDtypeStruct((CHUNKS * K, CHUNKS * K), BF16),
            jax.ShapeDtypeStruct((K, CHUNKS * K), BF16),
            jax.ShapeDtypeStruct((WIDE * QUARTER, CHUNKS * K), BF16),
        ],
        in_specs=[pl.BlockSpec(memory_space=pl.ANY), vmem],
        out_specs=[vmem, vmem, vmem],
        scratch_shapes=[*narrow_scratch(1), dma((CHUNKS,)), *[dma((1, CHUNKS))] * 6],
        compiler_params=pltpu.CompilerParams(
            collective_id=0, has_side_effects=True, vmem_limit_bytes=24 * 1024 * 1024
        ),
        name="first_projection",
    )(embeddings, ids)
    return pl.pallas_call(
        kernel,
        out_shape=jax.ShapeDtypeStruct((WIDE * SLOTS, K), BF16),
        in_specs=[vmem, vmem, vmem],
        out_specs=vmem,
        scratch_shapes=[
            *narrow_scratch(ITERS),
            pltpu.VMEM((CHUNKS, K, K), F32),
            pltpu.VMEM((K, CHUNKS * K), BF16),
            pltpu.VMEM((ITERS, RING - 1, PLANE, PIECE, K), BF16),
            pltpu.VMEM((ITERS, RING - 1, PLANE, PIECE, K), BF16),
            pltpu.VMEM((PLANE, PIECE, K), F32),
            pltpu.VMEM((ITERS, PLANE, PIECE, K), BF16),
            pltpu.VMEM((ITERS, PLANE, PIECE, K), BF16),
            pltpu.VMEM((RING, PIECE, K), F32),
            pltpu.VMEM((ITERS, WIDE, PIECE, K), BF16),
            pltpu.VMEM((2, HALF, K), F32),
            pltpu.VMEM((ITERS, HALF, K), F32),
            pltpu.VMEM((HALF, K), F32),
            pltpu.VMEM((ITERS, HALF, K), F32),
            pltpu.VMEM((ITERS, K, K), F32),
            pltpu.VMEM((HALF, 2 * HALF), F32),
            pltpu.VMEM((HALF, HALF), F32),
            pltpu.VMEM((K, K), F32),
            pltpu.VMEM((RING, PLANE, PIECE, HALF), BF16),
            pltpu.VMEM((4, 8, RING, 2, PIECE, HALF), BF16),
            pltpu.VMEM((WIDE * PIECE, HALF), F32),
            *[dma((ITERS, CHUNKS))] * 6,
            dma((ITERS,)),
            dma((ITERS, RING)),
            dma((ITERS,)),
            dma((ITERS,)),
            dma((ITERS,)),
            dma((ITERS, RING)),
            dma((ITERS,)),
            dma((ITERS, RING - 1)),
            dma((ITERS, 3)),
            dma((ITERS, 3)),
            dma,
            dma((RING,)),
            dma,
            dma((RING,)),
            dma,
            dma((2,)),
            dma,
        ],
        compiler_params=pltpu.CompilerParams(
            collective_id=1, has_side_effects=True, vmem_limit_bytes=40 * 1024 * 1024
        ),
        name="members",
    )(a, low, place)


def on_device(embeddings, cluster_ids):
    members = members_of(embeddings, cluster_ids.reshape(1, -1))
    count = members.shape[0] // lax.axis_size("narrow")
    own = lax.dynamic_slice_in_dim(members, lax.axis_index("narrow") * count, count, 0)
    return dot(members, own, NT).astype(BF16)[None]


def solution(mesh):
    return jax.shard_map(
        on_device,
        mesh=mesh,
        in_specs=(P("wide", "narrow"), P("wide", None)),
        out_specs=P("wide", None, "narrow"),
        check_vma=False,
    )
```

```python
import jax
import jax.numpy as jnp
from jax import lax
from jax.experimental import pallas as pl
from jax.experimental.pallas import tpu as pltpu
from jax.sharding import PartitionSpec as P

F32 = jnp.float32
BF16 = jnp.bfloat16
HIGHEST = lax.Precision.HIGHEST
MESH = pl.DeviceIdType.MESH

K = 256
ITERS = 2
HALF = 128
TRIANGLE = 192
PANEL = 16
CHUNKS = 4
WIDE = 64
PIECE = 16
SLOTS = 32
RING = 4
PLANE = 16
QUARTER = 8


def dot(a, b, dims, precision=None):
    return lax.dot_general(
        a, b, (dims, ((), ())), precision=precision, preferred_element_type=F32
    )


NN = ((1,), (0,))
NT = ((1,), (1,))


def split2(x):
    a = x.astype(BF16)
    return a, (x - a.astype(F32)).astype(BF16)


def split3(x):
    a = x.astype(BF16)
    b, c = split2(x - a.astype(F32))
    return a, b, c


def eliminate(m, between=None):
    n = HALF
    sub = lax.broadcasted_iota(jnp.int32, (PANEL, n), 0)
    for r0 in range(0, n, PANEL):
        left = m[r0 : r0 + PANEL, 0:n]
        right = m[r0 : r0 + PANEL, n : 2 * n]
        cols = [
            jnp.broadcast_to(left[:, r0 + j : r0 + j + 1], (PANEL, n)) for j in range(PANEL)
        ]
        scale = jnp.zeros((PANEL, n), F32)
        for j in range(PANEL):
            pivot = cols[j][j : j + 1, :]
            factor = jnp.where(sub > j, cols[j] * (1.0 / pivot), 0.0)
            for k in range(j + 1, PANEL):
                cols[k] = cols[k] - factor * cols[k][j : j + 1, :]
            left = left - factor * left[j : j + 1, :]
            right = right - factor * right[j : j + 1, :]
            scale = jnp.where(sub == j, lax.rsqrt(jnp.broadcast_to(pivot, (PANEL, n))), scale)
        left = left * scale
        right = right * scale
        m[r0 : r0 + PANEL, 0:n] = left
        m[r0 : r0 + PANEL, n : 2 * n] = right
        r1 = r0 + PANEL
        if r1 < n:
            a, b, c = (t.astype(F32) for t in split3(jnp.concatenate([left, right], axis=1)))
            rows = jnp.concatenate([a, a, b, b, a, c], axis=0)[:, 0:n].T[r1:].astype(BF16)
            pivots = jnp.concatenate([a, b, a, b, c, a], axis=0).astype(BF16)
            m[r1:n, :] = m[r1:n, :] - dot(rows, pivots, NN)
        if between is not None:
            between(r0 // PANEL)


def inverse_factor_start(square, m, out, cross):
    n = HALF
    row = lax.broadcasted_iota(jnp.int32, (n, n), 0)
    col = lax.broadcasted_iota(jnp.int32, (n, n), 1)
    eye = jnp.where(row == col, 1.0, 0.0).astype(F32)
    m[:, 0:n] = square[0, 0:n]
    m[:, n : 2 * n] = eye
    eliminate(m)
    first = m[:, n : 2 * n]
    cornered = jnp.concatenate([square[0, n:], square[1, n:]], axis=0)
    lower = dot(cornered, first, NT, HIGHEST)
    out[0:n, 0:n] = first
    out[0:n, n:] = jnp.zeros((n, n), F32)
    cross[...] = dot(lower, first, NN, HIGHEST)
    m[:, 0:n] = square[1, 0:n] - dot(lower, lower, NT, HIGHEST)
    m[:, n : 2 * n] = eye


def inverse_factor_end(m, out, cross, between):
    n = HALF
    eliminate(m, between)
    second = m[:, n : 2 * n]
    out[n:, n:] = second
    out[n:, 0:n] = -dot(second, cross[...], NN, HIGHEST)


def to(src, dst, send, recv, wide, narrow):
    return pltpu.make_async_remote_copy(
        src_ref=src,
        dst_ref=dst,
        send_sem=send,
        recv_sem=recv,
        device_id={"wide": wide, "narrow": narrow},
        device_id_type=MESH,
    )


def settle(block, sem):
    pltpu.make_async_copy(block, block, sem).wait()


def signal(barrier, wide, narrow):
    pl.semaphore_signal(
        barrier, inc=1, device_id={"wide": wide, "narrow": narrow}, device_id_type=MESH
    )


def sum_over_narrow(w, n, vt, a_ref, part, recv1, chip, send2, recv2, full, sems):
    core = lax.rem(n, 2)
    other = 1 - core
    core_peer = n + 1 - 2 * core
    chip_peer = lax.rem(n + 2, 4)
    s1, q1, s2, q2, s3, q3 = sems

    def c1(it, g):
        return to(part.at[g, other], recv1.at[it, g], s1.at[it, g], q1.at[it, g], w, core_peer)

    def c2(it, g):
        return to(send2.at[it, g], recv2.at[it, g], s2.at[it, g], q2.at[it, g], w, chip_peer)

    def c3(it, g, half):
        block = full.at[it, g, half]
        return to(block, block, s3.at[it, g], q3.at[it, g], w, core_peer)

    def project(it, g):
        now = dot(vt[...], a_ref[g * K : (g + 1) * K, :], NT)
        part[g, 0] = now[0:HALF]
        part[g, 1] = now[HALF:]
        c1(it, g).start()

    def over_cores(it, g):
        c1(it, g).wait_recv()
        now = part[g, core] + recv1[it, g]
        chip[g] = now
        send2[it, g] = now.astype(BF16)
        c2(it, g).start()

    def over_chips(it, g):
        c2(it, g).wait_recv()
        full[it, g, core] = chip[g] + recv2[it, g].astype(F32)
        c3(it, g, core).start()

    def whole(it, g):
        c3(it, g, other).wait_recv()
        return jnp.concatenate([full[it, g, 0], full[it, g, 1]], axis=0)

    def sent(it):
        for g in range(CHUNKS):
            c1(it, g).wait_send()
            c2(it, g).wait_send()
            c3(it, g, core).wait_send()

    return project, over_cores, over_chips, whole, sent


def kernel(
    a_hbm,
    ids_hbm,
    out_ref,
    a_ref,
    ids_ref,
    place,
    vt,
    part,
    recv1,
    chip,
    send2,
    recv2,
    full,
    coords,
    low,
    ys,
    yr1,
    own,
    ysb,
    yr2,
    mine4,
    yg,
    sq,
    sqr1,
    sqt,
    sqr2,
    sqf,
    work,
    cross,
    linv,
    outgoing,
    arrived,
    by_lane,
    load_sem,
    s1,
    q1,
    s2,
    q2,
    s3,
    q3,
    as_,
    aq,
    bs,
    bq,
    cs,
    cq,
    ds,
    dq,
    es,
    eq,
    ts,
    tq,
    vs,
    vq,
    fs,
    fq,
    gs,
):
    w = lax.axis_index("wide")
    n = lax.axis_index("narrow")
    core = lax.rem(n, 2)
    other = 1 - core
    core_peer = n + 1 - 2 * core
    chip_peer = lax.rem(n + 2, 4)
    z = w // 8
    y = lax.rem(w // 2, RING)
    x = lax.rem(w, 2)
    plane = z * 2 + x
    quad = z // 2
    within = lax.rem(plane, RING)

    def at(there, ring):
        return (there // 2) * 8 + ring * 2 + lax.rem(there, 2)

    barrier = pltpu.get_barrier_semaphore()

    @pl.loop(1, PLANE)
    def _(t):
        signal(barrier, at(lax.rem(plane + t, PLANE), y), n)

    for off in range(1, RING):
        signal(barrier, at(plane, lax.rem(y + off, RING)), n)
    signal(barrier, w, core_peer)
    signal(barrier, w, chip_peer)
    def load(g):
        piece = pl.ds(g * K, K)
        return pltpu.make_async_copy(a_hbm.at[piece], a_ref.at[piece], load_sem.at[g])

    for g in range(CHUNKS):
        load(g).start()
    load_ids = pltpu.make_async_copy(ids_hbm, ids_ref, load_sem.at[CHUNKS])
    load_ids.start()
    row = lax.broadcasted_iota(jnp.int32, (K, K), 0)
    col = lax.broadcasted_iota(jnp.int32, (K, K), 1)
    eye = jnp.where(row == col, 1.0, 0.0).astype(BF16)
    for g in range(CHUNKS):
        vt[:, g * K : (g + 1) * K] = eye
    project, over_cores, over_chips, whole, sent = sum_over_narrow(
        w, n, vt, a_ref, part, recv1, chip, send2, recv2, full, (s1, q1, s2, q2, s3, q3)
    )
    for g in range(CHUNKS):
        load(g).wait()
    pl.semaphore_wait(barrier, PLANE - 1 + RING - 1 + 2)
    for g in range(CHUNKS):
        project(0, g)
    for g in range(CHUNKS):
        over_cores(0, g)
    rows = a_ref.shape[0]
    load_ids.wait()
    ids = ids_ref[...]
    cluster = lax.broadcasted_iota(jnp.int32, (WIDE, rows), 0)
    onehot = jnp.where(cluster == ids, 1.0, 0.0).astype(F32)
    earlier = jnp.where(
        lax.broadcasted_iota(jnp.int32, (rows, rows), 0)
        < lax.broadcasted_iota(jnp.int32, (rows, rows), 1),
        1.0,
        0.0,
    ).astype(BF16)
    counts = dot(onehot.astype(BF16), earlier, NN)
    slot = jnp.sum(counts * onehot, axis=0, keepdims=True).astype(jnp.int32)
    offset = slot - n * QUARTER
    owner = ((ids >> 1) & 3) * PLANE + (ids >> 3) * 2 + (ids & 1)
    target = jnp.where((offset >= 0) & (offset < QUARTER), owner * QUARTER + offset, -1)

    @pl.loop(0, WIDE * QUARTER, step=128)
    def _(r):
        position = lax.broadcasted_iota(jnp.int32, (128, rows), 0) + r
        place[pl.ds(r, 128), :] = jnp.where(position == target, 1.0, 0.0).astype(BF16)
    for g in range(CHUNKS):
        over_chips(0, g)
    for g in range(CHUNKS):
        low[:, g * K : (g + 1) * K] = whole(0, g).astype(BF16)
    sent(0)

    def sweep(it, carry):
        def first(off, c, k):
            piece = pl.ds(c * RING, RING)
            return to(
                ys.at[it, off - 1, piece],
                yr1.at[it, off - 1, piece],
                as_.at[it],
                aq.at[it, k],
                at(plane, lax.rem(y + off, RING)),
                n,
            )

        order = (2, 1, 3, 0)
        for off in order:
            q = lax.rem(y + off, RING)
            now = dot(low[...], a_ref[:, pl.ds(pl.multiple_of(q * K, K), K)], NN)
            if off:
                ys[it, off - 1] = now.astype(BF16).reshape(PLANE, PIECE, K)
            else:
                own[...] = now.reshape(PLANE, PIECE, K)
            if off == 3:
                for k, turn in enumerate(order):
                    for there in (2, 1, 3):
                        first(there, lax.rem(quad + turn, RING), k).start()

        for k, turn in enumerate(order):
            c = lax.rem(quad + turn, RING)
            settle(yr1.at[it, :, pl.ds(0, RING)], aq.at[it, k])
            piece = pl.ds(c * RING, RING)
            now = own[piece]
            for off in (1, 2, 3):
                now = now + yr1[it, off - 1, piece].astype(F32)
            ysb[it, piece] = now.astype(BF16)
            if turn == 0:
                mine4[...] = now
            for t in range(0 if turn else 1, RING):
                there = c * RING + lax.rem(within + t, RING)
                to(ysb.at[it, there], yr2.at[it, plane], bs.at[it], bq.at[it], at(there, y), n).start()
        settle(yr2.at[it, pl.ds(0, PLANE - 1)], bq.at[it])
        total = mine4[within]
        for t in range(1, PLANE):
            total = total + yr2[it, lax.rem(plane + t, PLANE)].astype(F32)
        mine = yg.at[it, y * PLANE + plane]
        mine[...] = total.astype(BF16)

        @pl.loop(1, PLANE)
        def _(t):
            there = lax.rem(plane + t, PLANE)
            block = yg.at[it, y * PLANE + plane]
            to(block, block, cs.at[it], cq.at[it, quad], at(there, y), n).start()

        for turn in (0, 1, 3, 2):
            c = lax.rem(quad + turn, RING)
            settle(yg.at[it, pl.ds(0, RING if turn else RING - 1)], cq.at[it, c])
            block = yg.at[it, pl.ds(y * PLANE + c * RING, RING)]
            for off in (2, 1, 3):
                ring = lax.rem(y + off, RING)
                to(block, block, ds.at[it], dq.at[it, off - 1], at(plane, ring), n).start()
        for off in (0, 1, 3, 2):
            q = lax.rem(y - off + RING, RING)
            if off:
                settle(yg.at[it, pl.ds(0, PLANE)], dq.at[it, off - 1])
            vt[:, pl.ds(pl.multiple_of(q * K, K), K)] = yg[it, pl.ds(q * PLANE, PLANE)].reshape(K, K)

        now = dot(vt[...], vt[...], NT)
        sq[0, 0:HALF] = now[0:HALF, 0:HALF]
        sq[0, HALF:] = now[HALF : HALF + HALF // 2, 0:HALF]
        sq[1, 0:HALF] = now[HALF:, HALF:]
        sq[1, HALF:] = now[HALF + HALF // 2 :, 0:HALF]
        e1 = to(sq.at[other], sqr1.at[it], es.at[it, 0], eq.at[it, 0], w, core_peer)
        e1.start()
        e1.wait_recv()
        sqt[...] = sq[core] + sqr1[it]
        e2 = to(sqt, sqr2.at[it], es.at[it, 1], eq.at[it, 1], w, chip_peer)
        e2.start()
        for g in range(CHUNKS):
            project(it + 1, g)
        e2.wait_recv()
        half = sqf.at[it, core]
        half[...] = sqt[...] + sqr2[it]
        e3 = to(half, half, es.at[it, 2], eq.at[it, 2], w, core_peer)
        e3.start()
        for g in range(CHUNKS):
            over_cores(it + 1, g)
        rest = sqf.at[it, other]
        to(rest, rest, es.at[it, 2], eq.at[it, 2], w, core_peer).wait_recv()
        inverse_factor_start(sqf.at[it], work, linv, cross)


        def between(panel):
            if panel in (3, 4, 5, 6):
                over_chips(it + 1, panel - 3)

        inverse_factor_end(work, linv, cross, between)
        a, b = split2(linv[...])
        for g in range(CHUNKS):
            c, d = split2(whole(it + 1, g))
            now = dot(a, c, NN) + (dot(a, d, NN) + dot(b, c, NN))
            coords[g] = now
            low[:, g * K : (g + 1) * K] = now.astype(BF16)

        sent(it + 1)
        e1.wait_send()
        e2.wait_send()
        e3.wait_send()
        settle(ys.at[it], as_.at[it])
        settle(ysb.at[it, pl.ds(0, PLANE - 1)], bs.at[it])
        settle(yg.at[it, pl.ds(0, PLANE - 1)], cs.at[it])
        settle(ys.at[it], ds.at[it])
        return carry

    lax.fori_loop(0, ITERS, sweep, 0)

    for g in range(CHUNKS):
        now = coords[g]
        scale = lax.rsqrt(jnp.sum(now * now, axis=0, keepdims=True) + 1e-06)
        low[:, g * K : (g + 1) * K] = (now * scale).astype(BF16)
    now = dot(place[...], low[...], NT).reshape(RING, PLANE, QUARTER, K)
    outgoing[...] = jnp.concatenate([now[..., 0:HALF], now[..., HALF:]], axis=2).astype(BF16)

    for turn in (0, 1, 3, 2):
        c = lax.rem(quad + turn, RING)

        @pl.loop(0, PLANE)
        def _(t):
            ring = lax.rem(y + t, RING)
            there = c * RING + lax.rem(within + t // RING, RING)

            def send():
                to(
                    outgoing.at[ring, there],
                    arrived.at[n, z, y, x],
                    ts,
                    tq.at[quad],
                    at(there, ring),
                    n,
                ).start()

            if turn == 0:
                pl.when(t > 0)(send)
            else:
                send()

    arrived[n, z, y, x] = outgoing[y, plane]

    def share(c, who, peer, send, recv):
        block = arrived.at[who, pl.ds(c * 2, 2)]
        return to(block, block, send, recv, w, peer)

    for turn in (0, 1, 3, 2):
        c = lax.rem(quad + turn, RING)
        count = PLANE if turn else PLANE - 1
        settle(outgoing.at[0, pl.ds(0, count)], tq.at[c])
        share(c, n, chip_peer, vs, vq.at[c]).start()
        share(c, n, core_peer, fs, fq.at[0]).start()

    def arrange(who):
        by_lane[...] = arrived[who].astype(F32).reshape(WIDE * PIECE, HALF)
        for h in range(2):
            for s in range(QUARTER):
                out_ref[
                    pl.ds((who * QUARTER + s) * WIDE, WIDE), h * HALF : (h + 1) * HALF
                ] = by_lane[pl.ds(h * QUARTER + s, WIDE, stride=PIECE), :].astype(BF16)

    arrange(n)
    for turn in (0, 1, 3, 2):
        c = lax.rem(quad + turn, RING)
        share(c, chip_peer, chip_peer, vs, vq.at[c]).wait_recv()
        share(c, chip_peer, core_peer, gs, fq.at[1]).start()
    settle(arrived.at[core_peer], fq.at[0])
    arrange(core_peer)
    arrange(chip_peer)
    last = lax.rem(core_peer + 2, 4)
    settle(arrived.at[last], fq.at[1])
    arrange(last)
    settle(arrived.at[n], fs)
    settle(arrived.at[n], vs)
    settle(arrived.at[n], gs)
    for _ in range(RING - 1):
        settle(outgoing.at[0], ts)
    settle(outgoing.at[0, pl.ds(0, PLANE - 1)], ts)


def members_of(embeddings, ids):
    dma = pltpu.SemaphoreType.DMA
    vmem = pl.BlockSpec(memory_space=pltpu.VMEM)

    def narrow_scratch(times):
        return [
            pltpu.VMEM((K, CHUNKS * K), BF16),
            pltpu.VMEM((CHUNKS, 2, HALF, K), F32),
            pltpu.VMEM((times, CHUNKS, HALF, K), F32),
            pltpu.VMEM((CHUNKS, HALF, K), F32),
            pltpu.VMEM((times, CHUNKS, HALF, K), BF16),
            pltpu.VMEM((times, CHUNKS, HALF, K), BF16),
            pltpu.VMEM((times, CHUNKS, 2, HALF, K), F32),
        ]

    return pl.pallas_call(
        kernel,
        out_shape=jax.ShapeDtypeStruct((WIDE * SLOTS, K), BF16),
        in_specs=[pl.BlockSpec(memory_space=pl.ANY), pl.BlockSpec(memory_space=pl.ANY)],
        out_specs=vmem,
        scratch_shapes=[
            pltpu.VMEM((CHUNKS * K, CHUNKS * K), BF16),
            pltpu.VMEM((1, CHUNKS * K), jnp.int32),
            pltpu.VMEM((WIDE * QUARTER, CHUNKS * K), BF16),
            *narrow_scratch(ITERS + 1),
            pltpu.VMEM((CHUNKS, K, K), F32),
            pltpu.VMEM((K, CHUNKS * K), BF16),
            pltpu.VMEM((ITERS, RING - 1, PLANE, PIECE, K), BF16),
            pltpu.VMEM((ITERS, RING - 1, PLANE, PIECE, K), BF16),
            pltpu.VMEM((PLANE, PIECE, K), F32),
            pltpu.VMEM((ITERS, PLANE, PIECE, K), BF16),
            pltpu.VMEM((ITERS, PLANE, PIECE, K), BF16),
            pltpu.VMEM((RING, PIECE, K), F32),
            pltpu.VMEM((ITERS, WIDE, PIECE, K), BF16),
            pltpu.VMEM((2, TRIANGLE, HALF), F32),
            pltpu.VMEM((ITERS, TRIANGLE, HALF), F32),
            pltpu.VMEM((TRIANGLE, HALF), F32),
            pltpu.VMEM((ITERS, TRIANGLE, HALF), F32),
            pltpu.VMEM((ITERS, 2, TRIANGLE, HALF), F32),
            pltpu.VMEM((HALF, 2 * HALF), F32),
            pltpu.VMEM((HALF, HALF), F32),
            pltpu.VMEM((K, K), F32),
            pltpu.VMEM((RING, PLANE, PIECE, HALF), BF16),
            pltpu.VMEM((4, 8, RING, 2, PIECE, HALF), BF16),
            pltpu.VMEM((WIDE * PIECE, HALF), F32),
            dma((CHUNKS + 1,)),
            *[dma((ITERS + 1, CHUNKS))] * 6,
            dma((ITERS,)),
            dma((ITERS, RING)),
            dma((ITERS,)),
            dma((ITERS,)),
            dma((ITERS,)),
            dma((ITERS, RING)),
            dma((ITERS,)),
            dma((ITERS, RING - 1)),
            dma((ITERS, 3)),
            dma((ITERS, 3)),
            dma,
            dma((RING,)),
            dma,
            dma((RING,)),
            dma,
            dma((2,)),
            dma,
        ],
        compiler_params=pltpu.CompilerParams(
            collective_id=0, has_side_effects=True, vmem_limit_bytes=56 * 1024 * 1024
        ),
        name="members",
    )(embeddings, ids)


def on_device(embeddings, cluster_ids):
    members = members_of(embeddings, cluster_ids.reshape(1, -1))
    count = members.shape[0] // lax.axis_size("narrow")
    own = lax.dynamic_slice_in_dim(members, lax.axis_index("narrow") * count, count, 0)
    return dot(members, own, NT).astype(BF16)[None]


def solution(mesh):
    return jax.shard_map(
        on_device,
        mesh=mesh,
        in_specs=(P("wide", "narrow"), P("wide", None)),
        out_specs=P("wide", None, "narrow"),
        check_vma=False,
    )
```

```python
import jax
import jax.numpy as jnp
from jax import lax
from jax.experimental import pallas as pl
from jax.experimental.pallas import tpu as pltpu
from jax.sharding import PartitionSpec as P

F32 = jnp.float32
BF16 = jnp.bfloat16
HIGHEST = lax.Precision.HIGHEST
MESH = pl.DeviceIdType.MESH

K = 256
ITERS = 2
HALF = 128
TRIANGLE = 192
PANEL = 16
CHUNKS = 4
WIDE = 64
PIECE = 16
SLOTS = 32
RING = 4
PLANE = 16
QUARTER = 8


def dot(a, b, dims, precision=None):
    return lax.dot_general(
        a, b, (dims, ((), ())), precision=precision, preferred_element_type=F32
    )


NN = ((1,), (0,))
NT = ((1,), (1,))


def split2(x):
    a = x.astype(BF16)
    return a, (x - a.astype(F32)).astype(BF16)


def split3(x):
    a = x.astype(BF16)
    b, c = split2(x - a.astype(F32))
    return a, b, c


def eliminate(m, between=None):
    n = HALF
    sub = lax.broadcasted_iota(jnp.int32, (PANEL, n), 0)
    for r0 in range(0, n, PANEL):
        left = m[r0 : r0 + PANEL, 0:n]
        right = m[r0 : r0 + PANEL, n : 2 * n]
        cols = [
            jnp.broadcast_to(left[:, r0 + j : r0 + j + 1], (PANEL, n)) for j in range(PANEL)
        ]
        scale = jnp.zeros((PANEL, n), F32)
        for j in range(PANEL):
            pivot = cols[j][j : j + 1, :]
            factor = jnp.where(sub > j, cols[j] * (1.0 / pivot), 0.0)
            for k in range(j + 1, PANEL):
                cols[k] = cols[k] - factor * cols[k][j : j + 1, :]
            left = left - factor * left[j : j + 1, :]
            right = right - factor * right[j : j + 1, :]
            scale = jnp.where(sub == j, lax.rsqrt(jnp.broadcast_to(pivot, (PANEL, n))), scale)
        left = left * scale
        right = right * scale
        m[r0 : r0 + PANEL, 0:n] = left
        m[r0 : r0 + PANEL, n : 2 * n] = right
        r1 = r0 + PANEL
        if r1 < n:
            a, b, c = (t.astype(F32) for t in split3(jnp.concatenate([left, right], axis=1)))
            rows = jnp.concatenate([a, a, b, b, a, c], axis=0)[:, 0:n].T[r1:].astype(BF16)
            pivots = jnp.concatenate([a, b, a, b, c, a], axis=0).astype(BF16)
            m[r1:n, :] = m[r1:n, :] - dot(rows, pivots, NN)
        if between is not None:
            between(r0 // PANEL)


def inverse_factor_start(square, m, out, cross):
    n = HALF
    row = lax.broadcasted_iota(jnp.int32, (n, n), 0)
    col = lax.broadcasted_iota(jnp.int32, (n, n), 1)
    eye = jnp.where(row == col, 1.0, 0.0).astype(F32)
    m[:, 0:n] = square[0, 0:n]
    m[:, n : 2 * n] = eye
    eliminate(m)
    first = m[:, n : 2 * n]
    cornered = jnp.concatenate([square[0, n:], square[1, n:]], axis=0)
    lower = dot(cornered, first, NT, HIGHEST)
    out[0:n, 0:n] = first
    out[0:n, n:] = jnp.zeros((n, n), F32)
    cross[...] = dot(lower, first, NN, HIGHEST)
    m[:, 0:n] = square[1, 0:n] - dot(lower, lower, NT, HIGHEST)
    m[:, n : 2 * n] = eye


def inverse_factor_end(m, out, cross, between):
    n = HALF
    eliminate(m, between)
    second = m[:, n : 2 * n]
    out[n:, n:] = second
    out[n:, 0:n] = -dot(second, cross[...], NN, HIGHEST)


def to(src, dst, send, recv, wide, narrow):
    return pltpu.make_async_remote_copy(
        src_ref=src,
        dst_ref=dst,
        send_sem=send,
        recv_sem=recv,
        device_id={"wide": wide, "narrow": narrow},
        device_id_type=MESH,
    )


def settle(block, sem):
    pltpu.make_async_copy(block, block, sem).wait()


def signal(barrier, wide, narrow):
    pl.semaphore_signal(
        barrier, inc=1, device_id={"wide": wide, "narrow": narrow}, device_id_type=MESH
    )


def sum_over_narrow(w, n, vt, a_ref, part, recv1, chip, send2, recv2, full, sems):
    core = lax.rem(n, 2)
    other = 1 - core
    core_peer = n + 1 - 2 * core
    chip_peer = lax.rem(n + 2, 4)
    s1, q1, s2, q2, s3, q3 = sems

    def c1(it, g):
        return to(part.at[g, other], recv1.at[it, g], s1.at[it, g], q1.at[it, g], w, core_peer)

    def c2(it, g):
        return to(send2.at[it, g], recv2.at[it, g], s2.at[it, g], q2.at[it, g], w, chip_peer)

    def c3(it, g, half):
        block = full.at[it, g, half]
        return to(block, block, s3.at[it, g], q3.at[it, g], w, core_peer)

    def project(it, g):
        now = dot(vt[...], a_ref[g * K : (g + 1) * K, :], NT)
        part[g, 0] = now[0:HALF]
        part[g, 1] = now[HALF:]
        c1(it, g).start()

    def over_cores(it, g):
        c1(it, g).wait_recv()
        now = part[g, core] + recv1[it, g]
        chip[g] = now
        send2[it, g] = now.astype(BF16)
        c2(it, g).start()

    def over_chips(it, g):
        c2(it, g).wait_recv()
        full[it, g, core] = chip[g] + recv2[it, g].astype(F32)
        c3(it, g, core).start()

    def whole(it, g):
        c3(it, g, other).wait_recv()
        return jnp.concatenate([full[it, g, 0], full[it, g, 1]], axis=0)

    def sent(it):
        for g in range(CHUNKS):
            c1(it, g).wait_send()
            c2(it, g).wait_send()
            c3(it, g, core).wait_send()

    return project, over_cores, over_chips, whole, sent


def kernel(
    a_hbm,
    ids_hbm,
    out_ref,
    a_ref,
    ids_ref,
    place,
    vt,
    part,
    recv1,
    chip,
    send2,
    recv2,
    full,
    coords,
    low,
    ys,
    yr1,
    own,
    ysb,
    yr2,
    mine4,
    yg,
    sq,
    sqr1,
    sqt,
    sqr2,
    sqf,
    work,
    cross,
    linv,
    acc,
    outgoing,
    arrived,
    by_lane,
    load_sem,
    s1,
    q1,
    s2,
    q2,
    s3,
    q3,
    as_,
    aq,
    bs,
    bq,
    cs,
    cq,
    ds,
    dq,
    es,
    eq,
    ts,
    tq,
    vs,
    vq,
    fs,
    fq,
    gs,
):
    w = lax.axis_index("wide")
    n = lax.axis_index("narrow")
    core = lax.rem(n, 2)
    other = 1 - core
    core_peer = n + 1 - 2 * core
    chip_peer = lax.rem(n + 2, 4)
    z = w // 8
    y = lax.rem(w // 2, RING)
    x = lax.rem(w, 2)
    plane = z * 2 + x
    quad = z // 2
    within = lax.rem(plane, RING)

    def at(there, ring):
        return (there // 2) * 8 + ring * 2 + lax.rem(there, 2)

    barrier = pltpu.get_barrier_semaphore()

    @pl.loop(1, PLANE)
    def _(t):
        signal(barrier, at(lax.rem(plane + t, PLANE), y), n)

    for off in range(1, RING):
        signal(barrier, at(plane, lax.rem(y + off, RING)), n)
    signal(barrier, w, core_peer)
    signal(barrier, w, chip_peer)
    def load(g):
        piece = pl.ds(g * K, K)
        return pltpu.make_async_copy(a_hbm.at[piece], a_ref.at[piece], load_sem.at[g])

    for g in range(CHUNKS):
        load(g).start()
    load_ids = pltpu.make_async_copy(ids_hbm, ids_ref, load_sem.at[CHUNKS])
    load_ids.start()
    row = lax.broadcasted_iota(jnp.int32, (K, K), 0)
    col = lax.broadcasted_iota(jnp.int32, (K, K), 1)
    eye = jnp.where(row == col, 1.0, 0.0).astype(BF16)
    for g in range(CHUNKS):
        vt[:, g * K : (g + 1) * K] = eye
    project, over_cores, over_chips, whole, sent = sum_over_narrow(
        w, n, vt, a_ref, part, recv1, chip, send2, recv2, full, (s1, q1, s2, q2, s3, q3)
    )
    for g in range(CHUNKS):
        load(g).wait()
    pl.semaphore_wait(barrier, PLANE - 1 + RING - 1 + 2)
    for g in range(CHUNKS):
        project(0, g)
    for g in range(CHUNKS):
        over_cores(0, g)
    rows = a_ref.shape[0]
    load_ids.wait()
    ids = ids_ref[...]
    cluster = lax.broadcasted_iota(jnp.int32, (WIDE, rows), 0)
    onehot = jnp.where(cluster == ids, 1.0, 0.0).astype(F32)
    earlier = jnp.where(
        lax.broadcasted_iota(jnp.int32, (rows, rows), 0)
        < lax.broadcasted_iota(jnp.int32, (rows, rows), 1),
        1.0,
        0.0,
    ).astype(BF16)
    counts = dot(onehot.astype(BF16), earlier, NN)
    slot = jnp.sum(counts * onehot, axis=0, keepdims=True).astype(jnp.int32)
    offset = slot - n * QUARTER
    owner = ((ids >> 1) & 3) * PLANE + (ids >> 3) * 2 + (ids & 1)
    target = jnp.where((offset >= 0) & (offset < QUARTER), owner * QUARTER + offset, -1)

    @pl.loop(0, WIDE * QUARTER, step=128)
    def _(r):
        position = lax.broadcasted_iota(jnp.int32, (128, rows), 0) + r
        place[pl.ds(r, 128), :] = jnp.where(position == target, 1.0, 0.0).astype(BF16)
    for g in range(CHUNKS):
        over_chips(0, g)
    for g in range(CHUNKS):
        low[:, g * K : (g + 1) * K] = whole(0, g).astype(BF16)
    sent(0)

    def sweep(it, carry):
        def first(off, c, k):
            piece = pl.ds(c * RING, RING)
            return to(
                ys.at[it, off - 1, piece],
                yr1.at[it, off - 1, piece],
                as_.at[it],
                aq.at[it, k],
                at(plane, lax.rem(y + off, RING)),
                n,
            )

        order = (2, 1, 3, 0)
        for off in order:
            q = lax.rem(y + off, RING)
            now = dot(low[...], a_ref[:, pl.ds(pl.multiple_of(q * K, K), K)], NN)
            if off:
                ys[it, off - 1] = now.astype(BF16).reshape(PLANE, PIECE, K)
            else:
                own[...] = now.reshape(PLANE, PIECE, K)
            if off == 3:
                for k, turn in enumerate(order):
                    for there in (2, 1, 3):
                        first(there, lax.rem(quad + turn, RING), k).start()

        for k, turn in enumerate(order):
            c = lax.rem(quad + turn, RING)
            settle(yr1.at[it, :, pl.ds(0, RING)], aq.at[it, k])
            piece = pl.ds(c * RING, RING)
            now = own[piece]
            for off in (1, 2, 3):
                now = now + yr1[it, off - 1, piece].astype(F32)
            ysb[it, piece] = now.astype(BF16)
            if turn == 0:
                mine4[...] = now
            for t in range(0 if turn else 1, RING):
                there = c * RING + lax.rem(within + t, RING)
                to(ysb.at[it, there], yr2.at[it, plane], bs.at[it], bq.at[it], at(there, y), n).start()
        settle(yr2.at[it, pl.ds(0, PLANE - 1)], bq.at[it])
        total = mine4[within]
        for t in range(1, PLANE):
            total = total + yr2[it, lax.rem(plane + t, PLANE)].astype(F32)
        mine = yg.at[it, y * PLANE + plane]
        mine[...] = total.astype(BF16)

        @pl.loop(1, PLANE)
        def _(t):
            there = lax.rem(plane + t, PLANE)
            block = yg.at[it, y * PLANE + plane]
            to(block, block, cs.at[it], cq.at[it, quad], at(there, y), n).start()

        for turn in (0, 1, 3, 2):
            c = lax.rem(quad + turn, RING)
            settle(yg.at[it, pl.ds(0, RING if turn else RING - 1)], cq.at[it, c])
            block = yg.at[it, pl.ds(y * PLANE + c * RING, RING)]
            for off in (2, 1, 3):
                ring = lax.rem(y + off, RING)
                to(block, block, ds.at[it], dq.at[it, off - 1], at(plane, ring), n).start()
        for off in (0, 1, 3, 2):
            q = lax.rem(y - off + RING, RING)
            if off:
                settle(yg.at[it, pl.ds(0, PLANE)], dq.at[it, off - 1])
            block = yg[it, pl.ds(q * PLANE, PLANE)].reshape(K, K)
            vt[:, pl.ds(pl.multiple_of(q * K, K), K)] = block
            gram = dot(block, block, NT)
            if off == 2:
                now = acc[...] + gram
            elif off:
                acc[...] += gram
            else:
                acc[...] = gram

        sq[0, 0:HALF] = now[0:HALF, 0:HALF]
        sq[0, HALF:] = now[HALF : HALF + HALF // 2, 0:HALF]
        sq[1, 0:HALF] = now[HALF:, HALF:]
        sq[1, HALF:] = now[HALF + HALF // 2 :, 0:HALF]
        e1 = to(sq.at[other], sqr1.at[it], es.at[it, 0], eq.at[it, 0], w, core_peer)
        e1.start()
        e1.wait_recv()
        sqt[...] = sq[core] + sqr1[it]
        e2 = to(sqt, sqr2.at[it], es.at[it, 1], eq.at[it, 1], w, chip_peer)
        e2.start()
        for g in range(CHUNKS):
            project(it + 1, g)
        e2.wait_recv()
        half = sqf.at[it, core]
        half[...] = sqt[...] + sqr2[it]
        e3 = to(half, half, es.at[it, 2], eq.at[it, 2], w, core_peer)
        e3.start()
        for g in range(CHUNKS):
            over_cores(it + 1, g)
        rest = sqf.at[it, other]
        to(rest, rest, es.at[it, 2], eq.at[it, 2], w, core_peer).wait_recv()
        inverse_factor_start(sqf.at[it], work, linv, cross)


        def between(panel):
            if panel in (3, 4, 5, 6):
                over_chips(it + 1, panel - 3)

        inverse_factor_end(work, linv, cross, between)
        a, b = split2(linv[...])
        for g in range(CHUNKS):
            c, d = split2(whole(it + 1, g))
            now = dot(a, c, NN) + (dot(a, d, NN) + dot(b, c, NN))
            coords[g] = now
            low[:, g * K : (g + 1) * K] = now.astype(BF16)

        sent(it + 1)
        e1.wait_send()
        e2.wait_send()
        e3.wait_send()
        settle(ys.at[it], as_.at[it])
        settle(ysb.at[it, pl.ds(0, PLANE - 1)], bs.at[it])
        settle(yg.at[it, pl.ds(0, PLANE - 1)], cs.at[it])
        settle(ys.at[it], ds.at[it])
        return carry

    lax.fori_loop(0, ITERS, sweep, 0)

    for g in range(CHUNKS):
        now = coords[g]
        scale = lax.rsqrt(jnp.sum(now * now, axis=0, keepdims=True) + 1e-06)
        low[:, g * K : (g + 1) * K] = (now * scale).astype(BF16)
    now = dot(place[...], low[...], NT).reshape(RING, PLANE, QUARTER, K)
    outgoing[...] = jnp.concatenate([now[..., 0:HALF], now[..., HALF:]], axis=2).astype(BF16)

    for turn in (0, 1, 3, 2):
        c = lax.rem(quad + turn, RING)

        @pl.loop(0, PLANE)
        def _(t):
            ring = lax.rem(y + t, RING)
            there = c * RING + lax.rem(within + t // RING, RING)

            def send():
                to(
                    outgoing.at[ring, there],
                    arrived.at[n, z, y, x],
                    ts,
                    tq.at[quad],
                    at(there, ring),
                    n,
                ).start()

            if turn == 0:
                pl.when(t > 0)(send)
            else:
                send()

    arrived[n, z, y, x] = outgoing[y, plane]

    def share(c, who, peer, send, recv):
        block = arrived.at[who, pl.ds(c * 2, 2)]
        return to(block, block, send, recv, w, peer)

    for turn in (0, 1, 3, 2):
        c = lax.rem(quad + turn, RING)
        count = PLANE if turn else PLANE - 1
        settle(outgoing.at[0, pl.ds(0, count)], tq.at[c])
        share(c, n, chip_peer, vs, vq.at[c]).start()
        share(c, n, core_peer, fs, fq.at[0]).start()

    def arrange(who):
        by_lane[...] = arrived[who].astype(F32).reshape(WIDE * PIECE, HALF)
        for h in range(2):
            for s in range(QUARTER):
                out_ref[
                    pl.ds((who * QUARTER + s) * WIDE, WIDE), h * HALF : (h + 1) * HALF
                ] = by_lane[pl.ds(h * QUARTER + s, WIDE, stride=PIECE), :].astype(BF16)

    arrange(n)
    for turn in (0, 1, 3, 2):
        c = lax.rem(quad + turn, RING)
        share(c, chip_peer, chip_peer, vs, vq.at[c]).wait_recv()
        share(c, chip_peer, core_peer, gs, fq.at[1]).start()
    settle(arrived.at[core_peer], fq.at[0])
    arrange(core_peer)
    arrange(chip_peer)
    last = lax.rem(core_peer + 2, 4)
    settle(arrived.at[last], fq.at[1])
    arrange(last)
    settle(arrived.at[n], fs)
    settle(arrived.at[n], vs)
    settle(arrived.at[n], gs)
    for _ in range(RING - 1):
        settle(outgoing.at[0], ts)
    settle(outgoing.at[0, pl.ds(0, PLANE - 1)], ts)


def members_of(embeddings, ids):
    dma = pltpu.SemaphoreType.DMA
    vmem = pl.BlockSpec(memory_space=pltpu.VMEM)

    def narrow_scratch(times):
        return [
            pltpu.VMEM((K, CHUNKS * K), BF16),
            pltpu.VMEM((CHUNKS, 2, HALF, K), F32),
            pltpu.VMEM((times, CHUNKS, HALF, K), F32),
            pltpu.VMEM((CHUNKS, HALF, K), F32),
            pltpu.VMEM((times, CHUNKS, HALF, K), BF16),
            pltpu.VMEM((times, CHUNKS, HALF, K), BF16),
            pltpu.VMEM((times, CHUNKS, 2, HALF, K), F32),
        ]

    return pl.pallas_call(
        kernel,
        out_shape=jax.ShapeDtypeStruct((WIDE * SLOTS, K), BF16),
        in_specs=[pl.BlockSpec(memory_space=pl.ANY), pl.BlockSpec(memory_space=pl.ANY)],
        out_specs=vmem,
        scratch_shapes=[
            pltpu.VMEM((CHUNKS * K, CHUNKS * K), BF16),
            pltpu.VMEM((1, CHUNKS * K), jnp.int32),
            pltpu.VMEM((WIDE * QUARTER, CHUNKS * K), BF16),
            *narrow_scratch(ITERS + 1),
            pltpu.VMEM((CHUNKS, K, K), F32),
            pltpu.VMEM((K, CHUNKS * K), BF16),
            pltpu.VMEM((ITERS, RING - 1, PLANE, PIECE, K), BF16),
            pltpu.VMEM((ITERS, RING - 1, PLANE, PIECE, K), BF16),
            pltpu.VMEM((PLANE, PIECE, K), F32),
            pltpu.VMEM((ITERS, PLANE, PIECE, K), BF16),
            pltpu.VMEM((ITERS, PLANE, PIECE, K), BF16),
            pltpu.VMEM((RING, PIECE, K), F32),
            pltpu.VMEM((ITERS, WIDE, PIECE, K), BF16),
            pltpu.VMEM((2, TRIANGLE, HALF), F32),
            pltpu.VMEM((ITERS, TRIANGLE, HALF), F32),
            pltpu.VMEM((TRIANGLE, HALF), F32),
            pltpu.VMEM((ITERS, TRIANGLE, HALF), F32),
            pltpu.VMEM((ITERS, 2, TRIANGLE, HALF), F32),
            pltpu.VMEM((HALF, 2 * HALF), F32),
            pltpu.VMEM((HALF, HALF), F32),
            pltpu.VMEM((K, K), F32),
            pltpu.VMEM((K, K), F32),
            pltpu.VMEM((RING, PLANE, PIECE, HALF), BF16),
            pltpu.VMEM((4, 8, RING, 2, PIECE, HALF), BF16),
            pltpu.VMEM((WIDE * PIECE, HALF), F32),
            dma((CHUNKS + 1,)),
            *[dma((ITERS + 1, CHUNKS))] * 6,
            dma((ITERS,)),
            dma((ITERS, RING)),
            dma((ITERS,)),
            dma((ITERS,)),
            dma((ITERS,)),
            dma((ITERS, RING)),
            dma((ITERS,)),
            dma((ITERS, RING - 1)),
            dma((ITERS, 3)),
            dma((ITERS, 3)),
            dma,
            dma((RING,)),
            dma,
            dma((RING,)),
            dma,
            dma((2,)),
            dma,
        ],
        compiler_params=pltpu.CompilerParams(
            collective_id=0, has_side_effects=True, vmem_limit_bytes=56 * 1024 * 1024
        ),
        name="members",
    )(embeddings, ids)


def on_device(embeddings, cluster_ids):
    members = members_of(embeddings, cluster_ids.reshape(1, -1))
    count = members.shape[0] // lax.axis_size("narrow")
    own = lax.dynamic_slice_in_dim(members, lax.axis_index("narrow") * count, count, 0)
    return dot(members, own, NT).astype(BF16)[None]


def solution(mesh):
    return jax.shard_map(
        on_device,
        mesh=mesh,
        in_specs=(P("wide", "narrow"), P("wide", None)),
        out_specs=P("wide", None, "narrow"),
        check_vma=False,
    )
```

```python
import jax
import jax.numpy as jnp
from jax import lax
from jax.experimental import pallas as pl
from jax.experimental.pallas import tpu as pltpu
from jax.sharding import PartitionSpec as P

F32 = jnp.float32
BF16 = jnp.bfloat16
HIGHEST = lax.Precision.HIGHEST
MESH = pl.DeviceIdType.MESH

K = 256
ITERS = 2
HALF = 128
TRIANGLE = 192
PANEL = 16
CHUNKS = 4
WIDE = 64
PIECE = 16
SLOTS = 32
RING = 4
PLANE = 16
QUARTER = 8
LAYERS = 8


def dot(a, b, dims, precision=None):
    return lax.dot_general(
        a, b, (dims, ((), ())), precision=precision, preferred_element_type=F32
    )


NN = ((1,), (0,))
NT = ((1,), (1,))


def split2(x):
    a = x.astype(BF16)
    return a, (x - a.astype(F32)).astype(BF16)


def split3(x):
    a = x.astype(BF16)
    b, c = split2(x - a.astype(F32))
    return a, b, c


def eliminate(m, between=None):
    n = HALF
    sub = lax.broadcasted_iota(jnp.int32, (PANEL, n), 0)
    for r0 in range(0, n, PANEL):
        left = m[r0 : r0 + PANEL, 0:n]
        right = m[r0 : r0 + PANEL, n : 2 * n]
        cols = [
            jnp.broadcast_to(left[:, r0 + j : r0 + j + 1], (PANEL, n)) for j in range(PANEL)
        ]
        scale = jnp.zeros((PANEL, n), F32)
        for j in range(PANEL):
            pivot = cols[j][j : j + 1, :]
            factor = jnp.where(sub > j, cols[j] * (1.0 / pivot), 0.0)
            for k in range(j + 1, PANEL):
                cols[k] = cols[k] - factor * cols[k][j : j + 1, :]
            left = left - factor * left[j : j + 1, :]
            right = right - factor * right[j : j + 1, :]
            scale = jnp.where(sub == j, lax.rsqrt(jnp.broadcast_to(pivot, (PANEL, n))), scale)
        left = left * scale
        right = right * scale
        m[r0 : r0 + PANEL, 0:n] = left
        m[r0 : r0 + PANEL, n : 2 * n] = right
        r1 = r0 + PANEL
        if r1 < n:
            a, b, c = (t.astype(F32) for t in split3(jnp.concatenate([left, right], axis=1)))
            rows = jnp.concatenate([a, a, b, b, a, c], axis=0)[:, 0:n].T[r1:].astype(BF16)
            pivots = jnp.concatenate([a, b, a, b, c, a], axis=0).astype(BF16)
            m[r1:n, :] = m[r1:n, :] - dot(rows, pivots, NN)
        if between is not None:
            between(r0 // PANEL)


def inverse_factor_start(square, m, out, cross):
    n = HALF
    row = lax.broadcasted_iota(jnp.int32, (n, n), 0)
    col = lax.broadcasted_iota(jnp.int32, (n, n), 1)
    eye = jnp.where(row == col, 1.0, 0.0).astype(F32)
    m[:, 0:n] = square[0, 0:n]
    m[:, n : 2 * n] = eye
    eliminate(m)
    first = m[:, n : 2 * n]
    cornered = jnp.concatenate([square[0, n:], square[1, n:]], axis=0)
    lower = dot(cornered, first, NT, HIGHEST)
    out[0:n, 0:n] = first
    out[0:n, n:] = jnp.zeros((n, n), F32)
    cross[...] = dot(lower, first, NN, HIGHEST)
    m[:, 0:n] = square[1, 0:n] - dot(lower, lower, NT, HIGHEST)
    m[:, n : 2 * n] = eye


def inverse_factor_end(m, out, cross, between):
    n = HALF
    eliminate(m, between)
    second = m[:, n : 2 * n]
    out[n:, n:] = second
    out[n:, 0:n] = -dot(second, cross[...], NN, HIGHEST)


def to(src, dst, send, recv, wide, narrow):
    return pltpu.make_async_remote_copy(
        src_ref=src,
        dst_ref=dst,
        send_sem=send,
        recv_sem=recv,
        device_id={"wide": wide, "narrow": narrow},
        device_id_type=MESH,
    )


def settle(block, sem):
    pltpu.make_async_copy(block, block, sem).wait()


def signal(barrier, wide, narrow):
    pl.semaphore_signal(
        barrier, inc=1, device_id={"wide": wide, "narrow": narrow}, device_id_type=MESH
    )


def sum_over_narrow(w, n, vt, a_ref, part, recv1, chip, send2, recv2, full, sems):
    core = lax.rem(n, 2)
    other = 1 - core
    core_peer = n + 1 - 2 * core
    chip_peer = lax.rem(n + 2, 4)
    s1, q1, s2, q2, s3, q3 = sems

    def c1(it, g):
        return to(part.at[g, other], recv1.at[it, g], s1.at[it, g], q1.at[it, g], w, core_peer)

    def c2(it, g):
        return to(send2.at[it, g], recv2.at[it, g], s2.at[it, g], q2.at[it, g], w, chip_peer)

    def c3(it, g, half):
        block = full.at[it, g, half]
        return to(block, block, s3.at[it, g], q3.at[it, g], w, core_peer)

    def project(it, g):
        now = dot(vt[...], a_ref[g * K : (g + 1) * K, :], NT)
        part[g, 0] = now[0:HALF]
        part[g, 1] = now[HALF:]
        c1(it, g).start()

    def over_cores(it, g):
        c1(it, g).wait_recv()
        now = part[g, core] + recv1[it, g]
        chip[g] = now
        send2[it, g] = now.astype(BF16)
        c2(it, g).start()

    def over_chips(it, g):
        c2(it, g).wait_recv()
        full[it, g, core] = chip[g] + recv2[it, g].astype(F32)
        c3(it, g, core).start()

    def whole(it, g):
        c3(it, g, other).wait_recv()
        return jnp.concatenate([full[it, g, 0], full[it, g, 1]], axis=0)

    def sent(it):
        for g in range(CHUNKS):
            c1(it, g).wait_send()
            c2(it, g).wait_send()
            c3(it, g, core).wait_send()

    return project, over_cores, over_chips, whole, sent


def kernel(
    a_hbm,
    ids_hbm,
    out_ref,
    a_ref,
    ids_ref,
    place,
    vt,
    part,
    recv1,
    chip,
    send2,
    recv2,
    full,
    coords,
    low,
    ys,
    yr1,
    own,
    ysb,
    yr2,
    mine4,
    yg,
    sq,
    sqr1,
    sqt,
    sqr2,
    sqf,
    work,
    cross,
    linv,
    acc,
    outgoing,
    arrived,
    by_lane,
    load_sem,
    s1,
    q1,
    s2,
    q2,
    s3,
    q3,
    as_,
    aq,
    bs,
    bq,
    cs,
    cq,
    ds,
    dq,
    es,
    eq,
    ts,
    tq,
    vs,
    vq,
    fs,
    fq,
    gs,
):
    w = lax.axis_index("wide")
    n = lax.axis_index("narrow")
    core = lax.rem(n, 2)
    other = 1 - core
    core_peer = n + 1 - 2 * core
    chip_peer = lax.rem(n + 2, 4)
    z = w // 8
    y = lax.rem(w // 2, RING)
    x = lax.rem(w, 2)
    plane = z * 2 + x
    quad = z // 2
    within = lax.rem(plane, RING)

    def at(there, ring):
        return (there // 2) * 8 + ring * 2 + lax.rem(there, 2)

    barrier = pltpu.get_barrier_semaphore()

    @pl.loop(1, PLANE)
    def _(t):
        signal(barrier, at(lax.rem(plane + t, PLANE), y), n)

    for off in range(1, RING):
        signal(barrier, at(plane, lax.rem(y + off, RING)), n)
    signal(barrier, w, core_peer)
    signal(barrier, w, chip_peer)
    def load(g):
        piece = pl.ds(g * K, K)
        return pltpu.make_async_copy(a_hbm.at[piece], a_ref.at[piece], load_sem.at[g])

    for g in range(CHUNKS):
        load(g).start()
    load_ids = pltpu.make_async_copy(ids_hbm, ids_ref, load_sem.at[CHUNKS])
    load_ids.start()
    row = lax.broadcasted_iota(jnp.int32, (K, K), 0)
    col = lax.broadcasted_iota(jnp.int32, (K, K), 1)
    eye = jnp.where(row == col, 1.0, 0.0).astype(BF16)
    for g in range(CHUNKS):
        vt[:, g * K : (g + 1) * K] = eye
    project, over_cores, over_chips, whole, sent = sum_over_narrow(
        w, n, vt, a_ref, part, recv1, chip, send2, recv2, full, (s1, q1, s2, q2, s3, q3)
    )
    for g in range(CHUNKS):
        load(g).wait()
    pl.semaphore_wait(barrier, PLANE - 1 + RING - 1 + 2)
    for g in range(CHUNKS):
        project(0, g)
    for g in range(CHUNKS):
        over_cores(0, g)
    rows = a_ref.shape[0]
    load_ids.wait()
    ids = ids_ref[...]
    cluster = lax.broadcasted_iota(jnp.int32, (WIDE, rows), 0)
    onehot = jnp.where(cluster == ids, 1.0, 0.0).astype(F32)
    earlier = jnp.where(
        lax.broadcasted_iota(jnp.int32, (rows, rows), 0)
        < lax.broadcasted_iota(jnp.int32, (rows, rows), 1),
        1.0,
        0.0,
    ).astype(BF16)
    counts = dot(onehot.astype(BF16), earlier, NN)
    slot = jnp.sum(counts * onehot, axis=0, keepdims=True).astype(jnp.int32)
    offset = slot - n * QUARTER
    owner = ((ids >> 1) & 3) * PLANE + (ids >> 3) * 2 + (ids & 1)
    target = jnp.where((offset >= 0) & (offset < QUARTER), owner * QUARTER + offset, -1)

    @pl.loop(0, WIDE * QUARTER, step=128)
    def _(r):
        position = lax.broadcasted_iota(jnp.int32, (128, rows), 0) + r
        place[pl.ds(r, 128), :] = jnp.where(position == target, 1.0, 0.0).astype(BF16)
    for g in range(CHUNKS):
        over_chips(0, g)
    for g in range(CHUNKS):
        low[:, g * K : (g + 1) * K] = whole(0, g).astype(BF16)
    sent(0)

    def sweep(it, carry):
        def first(off, c, k):
            piece = pl.ds(c * RING, RING)
            return to(
                ys.at[it, off - 1, piece],
                yr1.at[it, off - 1, piece],
                as_.at[it],
                aq.at[it, k],
                at(plane, lax.rem(y + off, RING)),
                n,
            )

        order = (2, 1, 3, 0)
        for off in order:
            q = lax.rem(y + off, RING)
            now = dot(low[...], a_ref[:, pl.ds(pl.multiple_of(q * K, K), K)], NN)
            if off:
                ys[it, off - 1] = now.astype(BF16).reshape(PLANE, PIECE, K)
            else:
                own[...] = now.reshape(PLANE, PIECE, K)
            if off == 3:
                for k, turn in enumerate(order):
                    for there in (2, 1, 3):
                        first(there, lax.rem(quad + turn, RING), k).start()

        for k, turn in enumerate(order):
            c = lax.rem(quad + turn, RING)
            settle(yr1.at[it, :, pl.ds(0, RING)], aq.at[it, k])
            piece = pl.ds(c * RING, RING)
            now = own[piece]
            for off in (1, 2, 3):
                now = now + yr1[it, off - 1, piece].astype(F32)
            ysb[it, piece] = now.astype(BF16)
            if turn == 0:
                mine4[...] = now
            for t in range(0 if turn else 1, RING):
                there = c * RING + lax.rem(within + t, RING)
                to(ysb.at[it, there], yr2.at[it, plane], bs.at[it], bq.at[it], at(there, y), n).start()
        settle(yr2.at[it, pl.ds(0, PLANE - 1)], bq.at[it])
        total = mine4[within]
        for t in range(1, PLANE):
            total = total + yr2[it, lax.rem(plane + t, PLANE)].astype(F32)
        mine = yg.at[it, y * PLANE + plane]
        mine[...] = total.astype(BF16)

        @pl.loop(1, PLANE)
        def _(t):
            there = lax.rem(plane + t, PLANE)
            block = yg.at[it, y * PLANE + plane]
            to(block, block, cs.at[it], cq.at[it, quad], at(there, y), n).start()

        for turn in (0, 1, 3, 2):
            c = lax.rem(quad + turn, RING)
            settle(yg.at[it, pl.ds(0, RING if turn else RING - 1)], cq.at[it, c])
            block = yg.at[it, pl.ds(y * PLANE + c * RING, RING)]
            for off in (2, 1, 3):
                ring = lax.rem(y + off, RING)
                to(block, block, ds.at[it], dq.at[it, off - 1], at(plane, ring), n).start()
        for off in (0, 1, 3, 2):
            q = lax.rem(y - off + RING, RING)
            if off:
                settle(yg.at[it, pl.ds(0, PLANE)], dq.at[it, off - 1])
            block = yg[it, pl.ds(q * PLANE, PLANE)].reshape(K, K)
            vt[:, pl.ds(pl.multiple_of(q * K, K), K)] = block
            gram = dot(block, block, NT)
            if off == 2:
                now = acc[...] + gram
            elif off:
                acc[...] += gram
            else:
                acc[...] = gram

        sq[0, 0:HALF] = now[0:HALF, 0:HALF]
        sq[0, HALF:] = now[HALF : HALF + HALF // 2, 0:HALF]
        sq[1, 0:HALF] = now[HALF:, HALF:]
        sq[1, HALF:] = now[HALF + HALF // 2 :, 0:HALF]
        e1 = to(sq.at[other], sqr1.at[it], es.at[it, 0], eq.at[it, 0], w, core_peer)
        e1.start()
        e1.wait_recv()
        sqt[...] = sq[core] + sqr1[it]
        e2 = to(sqt, sqr2.at[it], es.at[it, 1], eq.at[it, 1], w, chip_peer)
        e2.start()
        for g in range(CHUNKS):
            project(it + 1, g)
        e2.wait_recv()
        half = sqf.at[it, core]
        half[...] = sqt[...] + sqr2[it]
        e3 = to(half, half, es.at[it, 2], eq.at[it, 2], w, core_peer)
        e3.start()
        for g in range(CHUNKS):
            over_cores(it + 1, g)
        rest = sqf.at[it, other]
        to(rest, rest, es.at[it, 2], eq.at[it, 2], w, core_peer).wait_recv()
        inverse_factor_start(sqf.at[it], work, linv, cross)


        def between(panel):
            if panel in (3, 4, 5, 6):
                over_chips(it + 1, panel - 3)

        inverse_factor_end(work, linv, cross, between)
        a, b = split2(linv[...])
        for g in range(CHUNKS):
            c, d = split2(whole(it + 1, g))
            now = dot(a, c, NN) + (dot(a, d, NN) + dot(b, c, NN))
            coords[g] = now
            low[:, g * K : (g + 1) * K] = now.astype(BF16)

        sent(it + 1)
        e1.wait_send()
        e2.wait_send()
        e3.wait_send()
        settle(ys.at[it], as_.at[it])
        settle(ysb.at[it, pl.ds(0, PLANE - 1)], bs.at[it])
        settle(yg.at[it, pl.ds(0, PLANE - 1)], cs.at[it])
        settle(ys.at[it], ds.at[it])
        return carry

    lax.fori_loop(0, ITERS, sweep, 0)

    for g in range(CHUNKS):
        now = coords[g]
        scale = lax.rsqrt(jnp.sum(now * now, axis=0, keepdims=True) + 1e-06)
        low[:, g * K : (g + 1) * K] = (now * scale).astype(BF16)
    now = dot(place[...], low[...], NT).reshape(RING, PLANE, QUARTER, K)
    outgoing[...] = jnp.concatenate([now[..., 0:HALF], now[..., HALF:]], axis=2).astype(BF16)

    layers = (0, 1, 7, 2, 6, 3, 5, 4)
    for turn in layers:
        c = lax.rem(z + turn, LAYERS)

        @pl.loop(0, 2 * RING)
        def _(t):
            ring = lax.rem(y + t, RING)
            there = c * 2 + lax.rem(x + t // RING, 2)

            def send():
                to(
                    outgoing.at[ring, there],
                    arrived.at[n, z, y, x],
                    ts,
                    tq.at[z],
                    at(there, ring),
                    n,
                ).start()

            if turn == 0:
                pl.when(t > 0)(send)
            else:
                send()

    arrived[n, z, y, x] = outgoing[y, plane]

    def share(c, who, peer, send, recv):
        block = arrived.at[who, c]
        return to(block, block, send, recv, w, peer)

    for turn in layers:
        c = lax.rem(z + turn, LAYERS)
        count = 2 * RING if turn else 2 * RING - 1
        settle(outgoing.at[0, pl.ds(0, count)], tq.at[c])
        share(c, n, chip_peer, vs, vq.at[c]).start()
        share(c, n, core_peer, fs, fq.at[0]).start()

    def arrange(who):
        by_lane[...] = arrived[who].astype(F32).reshape(WIDE * PIECE, HALF)
        for h in range(2):
            for s in range(QUARTER):
                out_ref[
                    pl.ds((who * QUARTER + s) * WIDE, WIDE), h * HALF : (h + 1) * HALF
                ] = by_lane[pl.ds(h * QUARTER + s, WIDE, stride=PIECE), :].astype(BF16)

    arrange(n)
    for turn in layers:
        c = lax.rem(z + turn, LAYERS)
        share(c, chip_peer, chip_peer, vs, vq.at[c]).wait_recv()
        share(c, chip_peer, core_peer, gs, fq.at[1]).start()
    settle(arrived.at[core_peer], fq.at[0])
    arrange(core_peer)
    arrange(chip_peer)
    last = lax.rem(core_peer + 2, 4)
    settle(arrived.at[last], fq.at[1])
    arrange(last)
    settle(arrived.at[n], fs)
    settle(arrived.at[n], vs)
    settle(arrived.at[n], gs)
    for _ in range(RING - 1):
        settle(outgoing.at[0], ts)
    settle(outgoing.at[0, pl.ds(0, PLANE - 1)], ts)


def members_of(embeddings, ids):
    dma = pltpu.SemaphoreType.DMA
    vmem = pl.BlockSpec(memory_space=pltpu.VMEM)

    def narrow_scratch(times):
        return [
            pltpu.VMEM((K, CHUNKS * K), BF16),
            pltpu.VMEM((CHUNKS, 2, HALF, K), F32),
            pltpu.VMEM((times, CHUNKS, HALF, K), F32),
            pltpu.VMEM((CHUNKS, HALF, K), F32),
            pltpu.VMEM((times, CHUNKS, HALF, K), BF16),
            pltpu.VMEM((times, CHUNKS, HALF, K), BF16),
            pltpu.VMEM((times, CHUNKS, 2, HALF, K), F32),
        ]

    return pl.pallas_call(
        kernel,
        out_shape=jax.ShapeDtypeStruct((WIDE * SLOTS, K), BF16),
        in_specs=[pl.BlockSpec(memory_space=pl.ANY), pl.BlockSpec(memory_space=pl.ANY)],
        out_specs=vmem,
        scratch_shapes=[
            pltpu.VMEM((CHUNKS * K, CHUNKS * K), BF16),
            pltpu.VMEM((1, CHUNKS * K), jnp.int32),
            pltpu.VMEM((WIDE * QUARTER, CHUNKS * K), BF16),
            *narrow_scratch(ITERS + 1),
            pltpu.VMEM((CHUNKS, K, K), F32),
            pltpu.VMEM((K, CHUNKS * K), BF16),
            pltpu.VMEM((ITERS, RING - 1, PLANE, PIECE, K), BF16),
            pltpu.VMEM((ITERS, RING - 1, PLANE, PIECE, K), BF16),
            pltpu.VMEM((PLANE, PIECE, K), F32),
            pltpu.VMEM((ITERS, PLANE, PIECE, K), BF16),
            pltpu.VMEM((ITERS, PLANE, PIECE, K), BF16),
            pltpu.VMEM((RING, PIECE, K), F32),
            pltpu.VMEM((ITERS, WIDE, PIECE, K), BF16),
            pltpu.VMEM((2, TRIANGLE, HALF), F32),
            pltpu.VMEM((ITERS, TRIANGLE, HALF), F32),
            pltpu.VMEM((TRIANGLE, HALF), F32),
            pltpu.VMEM((ITERS, TRIANGLE, HALF), F32),
            pltpu.VMEM((ITERS, 2, TRIANGLE, HALF), F32),
            pltpu.VMEM((HALF, 2 * HALF), F32),
            pltpu.VMEM((HALF, HALF), F32),
            pltpu.VMEM((K, K), F32),
            pltpu.VMEM((K, K), F32),
            pltpu.VMEM((RING, PLANE, PIECE, HALF), BF16),
            pltpu.VMEM((4, 8, RING, 2, PIECE, HALF), BF16),
            pltpu.VMEM((WIDE * PIECE, HALF), F32),
            dma((CHUNKS + 1,)),
            *[dma((ITERS + 1, CHUNKS))] * 6,
            dma((ITERS,)),
            dma((ITERS, RING)),
            dma((ITERS,)),
            dma((ITERS,)),
            dma((ITERS,)),
            dma((ITERS, RING)),
            dma((ITERS,)),
            dma((ITERS, RING - 1)),
            dma((ITERS, 3)),
            dma((ITERS, 3)),
            dma,
            dma((LAYERS,)),
            dma,
            dma((LAYERS,)),
            dma,
            dma((2,)),
            dma,
        ],
        compiler_params=pltpu.CompilerParams(
            collective_id=0, has_side_effects=True, vmem_limit_bytes=56 * 1024 * 1024
        ),
        name="members",
    )(embeddings, ids)


def on_device(embeddings, cluster_ids):
    members = members_of(embeddings, cluster_ids.reshape(1, -1))
    count = members.shape[0] // lax.axis_size("narrow")
    own = lax.dynamic_slice_in_dim(members, lax.axis_index("narrow") * count, count, 0)
    return dot(members, own, NT).astype(BF16)[None]


def solution(mesh):
    return jax.shard_map(
        on_device,
        mesh=mesh,
        in_specs=(P("wide", "narrow"), P("wide", None)),
        out_specs=P("wide", None, "narrow"),
        check_vma=False,
    )
```
